128 devices in a mesh: dp: 2 (over core), row: 8 (over y, x_lo), col: 8 (over x_hi, z).
Axes of the slice: x: 4 (x_hi: 2, x_lo: 2; x = x_hi * 2 + x_lo), y: 4, z: 4, core: 2. Of those that a mesh axis runs over, the one named last changes fastest.
Arguments:
- tokens: bfloat16 [8192, 6144], P(('dp', 'row'), 'col'), may hold values from -6 to 6
- w_qkv: bfloat16 [6144, 9216], P(('dp', 'row'), 'col'), may hold values from -0.078125 to 0.078125
- w_out: bfloat16 [3072, 6144], P(('dp', 'row'), 'col'), may hold values from -0.109375 to 0.109375
- ada_shift: float32 [2, 6144], P('dp'), may hold values from -3 to 3
- ada_scale: float32 [2, 6144], P('dp'), may hold values from -3 to 3
- out_gate: float32 [2, 6144], P('dp', 'col'), may hold values from 0.5 to 2
- head_gain: float32 [24], P('col'), may hold values from 1 to 4
- block_segment: int32 [2, 32], P('dp'), may hold values from 0 to 7, never falling along the last dimension, each value on 1 to 16 neighbouring positions
Outputs:
- mixed: bfloat16 [8192, 6144], P(('dp', 'row'), 'col')
The draws below stay inside these ranges and needn't reach their ends.
Inputs may be any that keep to these rules, and one draw needn't show every extreme that they name: `block_segment`: in each replica's row the numbers never fall; each request covers 1 to 16 consecutive blocks, and one covers exactly 16.
All inputs are finite; a program needn't handle non-finite values.
Results may differ from the reference program's by a relative error of at most 0.01.
Values may be sent and summed in bfloat16 or wider, within the bound.
A program may use at most 128 MiB of HBM per device.

```python
import math
import jax
import jax.numpy as jnp
import numpy as np
from jax import lax

D = 6144
HEADS = 24
HD = 128
BLK = 128
TOK_DEV = 512
BLOCKS_REP = 32
TOKENS = 8192
N_DP = 2
N_ROW = 8


def steps_of(key, dims, split, low, top_value):
    def one(dim, shards_of):
        steps = jax.random.uniform(jax.random.fold_in(jax.random.fold_in(key, 6), dim), (shards_of,), jnp.float32, low / len(split), top_value / len(split))
        return jnp.repeat(jnp.exp(steps), dims[dim] // shards_of).reshape((-1,) + (1,) * (len(dims) - dim - 1))

    loudness = one(*split[0])
    for cut in split[1:]:
        loudness = loudness * one(*cut)
    return loudness


def length_profile(amount, total, reach, slope):
    weights = [(1 << 20) // math.isqrt(grade ** slope) + 1 for grade in range(2, amount + 1)]
    surplus, holding = total - reach - (amount - 1), [1] * (amount - 1)
    while surplus > 0:
        free = [i for i in range(amount - 1) if holding[i] < reach]
        pool, left = sum([weights[i] for i in free]), surplus
        for i in free:
            addition = min(reach - holding[i], max(1, left * weights[i] // pool), surplus)
            holding[i] = holding[i] + addition
            surplus = surplus - addition
    return np.array([reach] + holding)


def uneven_parts(own_key, amount, total, bound, lean):
    if amount == 2:
        one = jax.random.randint(own_key, (), max(1, total - bound), min(bound, total - 1) + 1)
        return jnp.stack([one, total - one])
    sizes = jnp.asarray(length_profile(amount, total, bound, lean), jnp.int32)
    couples = (amount - 1) // 2
    source_of, receiver = sizes[1:1 + 2 * couples:2], sizes[2:2 + 2 * couples:2]
    room = jnp.minimum(source_of - 1, bound - receiver)
    passed = jax.random.randint(jax.random.fold_in(own_key, 1), (couples,), 0, 1 << 20) % (room + 1)
    sizes = sizes.at[1:1 + 2 * couples:2].set(source_of - passed).at[2:2 + 2 * couples:2].set(receiver + passed)
    return sizes[jax.random.permutation(jax.random.fold_in(own_key, 2), amount)]


def noise(key, extent, width, reach, shards=(), held_as=jnp.bfloat16):
    loudness = steps_of(key, extent, shards, -0.22, 0.18) if shards else 1.0
    drawn = jax.random.normal(key, extent, jnp.float32) * width * loudness
    return jnp.minimum(jnp.maximum(drawn, -reach), reach).astype(held_as)


def setup_inputs(seed: int = 0) -> dict:
    arg_keys = jax.random.split(jax.random.key(seed), 9)
    tokens = noise(arg_keys[0], (TOKENS, D), 1.0, 6.0, ((0, 16), (1, 8)))
    w_qkv = noise(arg_keys[1], (D, 3 * HEADS * HD), D ** -0.5, 0.078125, ((0, 16), (1, 8)))
    w_out = noise(arg_keys[2], (HEADS * HD, D), (HEADS * HD) ** -0.5, 0.109375, ((0, 16), (1, 8)))
    ada_shift = noise(arg_keys[3], (N_DP, D), 0.5, 3.0, ((0, 2),), jnp.float32)
    ada_scale = noise(arg_keys[4], (N_DP, D), 0.5, 3.0, ((0, 2),), jnp.float32)
    out_gate = jnp.clip(jnp.exp(math.log(2.0) - 1.3862944 * jax.random.uniform(arg_keys[5], (N_DP, D), jnp.float32) ** steps_of(arg_keys[5], (N_DP, D), ((0, 2), (1, 8)), -0.2, 0.2)), 0.5, 2.0)
    head_gain = jnp.clip(jnp.exp(math.log(4.0) - 1.3862944 * jax.random.uniform(arg_keys[6], (HEADS,), jnp.float32) ** steps_of(arg_keys[6], (HEADS,), ((0, 8),), -0.2, 0.2)), 1.0, 4.0)
    block_segment = jax.vmap(lambda own: jnp.searchsorted(jnp.cumsum(uneven_parts(own, BLOCKS_REP // 4, BLOCKS_REP, BLOCKS_REP // 2, 0)), jnp.arange(BLOCKS_REP), side="right"))(jax.random.split(arg_keys[7], N_DP)).reshape((N_DP, BLOCKS_REP)).astype(jnp.int32)
    return dict(tokens=tokens, w_qkv=w_qkv, w_out=w_out, ada_shift=ada_shift, ada_scale=ada_scale, out_gate=out_gate, head_gain=head_gain, block_segment=block_segment)


def rms_norm(vector):
    return vector * lax.rsqrt(lax.optimization_barrier(jnp.mean(vector * vector, axis=-1, keepdims=True)) + 1e-06)

def reference(tokens, w_qkv, w_out, ada_shift, ada_scale, out_gate, head_gain, block_segment):
    per_replica = TOK_DEV * N_ROW
    inverse = 1.0 / HD ** 0.5
    results = []
    for replica in range(N_DP):
        x_float = tokens[replica * per_replica:(replica + 1) * per_replica].astype(jnp.float32)
        row_mean = lax.optimization_barrier(jnp.mean(x_float, axis=-1, keepdims=True))
        centred = x_float - row_mean
        variance = lax.optimization_barrier(jnp.mean(centred * centred, axis=-1, keepdims=True))
        normed = centred * lax.rsqrt(variance + 1e-06)
        modulated = (normed * (1.0 + ada_scale[replica]) + ada_shift[replica]).astype(jnp.bfloat16)
        projected = jnp.dot(modulated, w_qkv, preferred_element_type=jnp.float32)
        projected = projected.reshape(per_replica, HEADS, 3, HD)
        query = (rms_norm(projected[:, :, 0]) * head_gain[None, :, None]).astype(jnp.bfloat16)
        keys = rms_norm(projected[:, :, 1]).astype(jnp.bfloat16)
        values = projected[:, :, 2].astype(jnp.bfloat16)
        token_segment = jnp.repeat(block_segment[replica], BLK)
        same_mask = (token_segment[:, None] == token_segment[None, :]).astype(jnp.float32)

        def one_head(operands):
            q_head, k_head, v_head = operands
            scores = jnp.dot(q_head, k_head.T, preferred_element_type=jnp.float32) * inverse
            weights = jnp.exp(scores) * same_mask
            totals = lax.optimization_barrier(jnp.sum(weights, axis=-1))
            summed = jnp.dot(weights.astype(jnp.bfloat16), v_head, preferred_element_type=jnp.float32)
            return (summed / totals[:, None]).astype(jnp.bfloat16)
        attended = lax.map(one_head, (jnp.transpose(query, (1, 0, 2)), jnp.transpose(keys, (1, 0, 2)), jnp.transpose(values, (1, 0, 2))))
        attended = jnp.transpose(attended, (1, 0, 2)).reshape(per_replica, HEADS * HD)
        branch = jnp.dot(attended, w_out, preferred_element_type=jnp.float32)
        results.append((out_gate[replica] * branch).astype(jnp.bfloat16))
    return jnp.concatenate(results, axis=0)
```

```python
import math

import jax
import jax.numpy as jnp
from jax import lax
from jax.experimental import pallas as pl
from jax.experimental.pallas import tpu as pltpu
from jax.sharding import PartitionSpec as P

HD = 128
BLK = 128
EPS = 1e-06
FAR = 2048.0
F32 = jnp.float32
BF16 = jnp.bfloat16
MESH = pl.DeviceIdType.MESH
N_FLOWS = 136


class Net:
    def __init__(self, ss, rs):
        self.ss, self.rs, self.count, self.sent = ss, rs, 0, []

    def ids(self, amount):
        first = self.count
        self.count += amount
        assert self.count <= N_FLOWS
        return list(range(first, self.count))

    def copy(self, i, src, dst, device):
        return pltpu.make_async_remote_copy(
            src_ref=src,
            dst_ref=dst,
            send_sem=self.ss.at[i],
            recv_sem=self.rs.at[i],
            device_id=device,
            device_id_type=MESH,
        )

    def send(self, i, src, dst, device, keep=True):
        copy = self.copy(i, src, dst, device)
        copy.start()
        if keep:
            self.sent.append(copy)
        return copy

    def recv(self, i, ref, device):
        self.copy(i, ref, ref, device).wait_recv()


def kernel(
    tok, wq, wo, shift, scale, gate, gain, seg, out,
    G, Xg, kvx, qx, woG, attg, acc, oacc, bacc, mod, ast, st, segb, ss, rs, ls,
):
    d, row, c = lax.axis_index("dp"), lax.axis_index("row"), lax.axis_index("col")
    y, l = row // 2, row % 2
    h, z = c // 4, c % 4
    yn, yf, yb = (y + 1) % 4, (y + 2) % 4, (y + 3) % 4
    zn, zf, zb = (z + 1) % 4, (z + 2) % 4, (z + 3) % 4
    h2 = 1 - h
    core = (1 - d, row, c)
    xl = (d, 2 * y + 1 - l, c)
    yp, ym = (d, 2 * yn + l, c), (d, 2 * yb + l, c)
    zp, zm = (d, row, 4 * h + zn), (d, row, 4 * h + zb)
    xh = (d, row, 4 * h2 + z)
    sw = (l, 2 * y + d, c)
    rr = 2 * y + d
    net = Net(ss, rs)

    def both_sides(first, second):
        pl.when(d == l)(first)
        pl.when(d != l)(second)

    x = tok[...].astype(F32)
    part_mean = jnp.sum(x, axis=-1, keepdims=True) * (1.0 / 768.0)
    off = x - part_mean
    part_sq = jnp.sum(off * off, axis=-1, keepdims=True)
    lane = lax.broadcasted_iota(jnp.int32, (512, 128), 1)
    columns = jnp.where(lane == 0, part_mean, jnp.where(lane == 1, part_sq, 0.0))
    st[c] = columns.T[:8]
    for b in range(32):
        segb[0, b : b + 1, :] = jnp.full((1, 128), seg[0, b], jnp.int32).astype(F32)

    barrier = pltpu.get_barrier_semaphore()
    col_peers = [(d, row, (c + k) % 8) for k in range(1, 8)]
    for peer in col_peers + [core, xl, yp, ym]:
        pl.semaphore_signal(barrier, inc=1, device_id=peer, device_id_type=MESH)

    @pl.when(d != l)
    def _():
        pl.semaphore_signal(barrier, inc=1, device_id=sw, device_id_type=MESH)

    pl.semaphore_wait(barrier, 11 + (d + l) % 2)

    def wid(dd, yy, ll):
        return 8 * dd + 2 * yy + ll

    class Weight:
        def __init__(self, src, dst, rows, local_sem):
            self.src, self.dst, self.half = src, dst, rows // 2
            self.f = net.ids(17)
            self.local = pltpu.make_async_copy(src, dst.at[wid(d, y, l)], local_sem)

        def at(self, dd, yy, ll, part=None):
            ref = self.dst.at[wid(dd, yy, ll)]
            if part is None:
                return ref
            return ref.at[pl.ds(part * self.half, self.half)]

        def go(self, i, ref, device):
            net.send(self.f[i], ref, ref, device)

        def got(self, i, ref):
            net.recv(self.f[i], ref, core)

        def own(self):
            me = self.at(d, y, l)
            for i, device in ((1, yp), (2, ym), (0, xl), (3, core)):
                net.send(self.f[i], self.src, me, device)
            self.local.start()

        def first_ring(self):
            self.got(1, self.at(d, yb, l))
            self.go(7, self.at(d, yb, l, 0), yp)
            self.go(8, self.at(d, yb, l), core)
            self.got(2, self.at(d, yn, l))
            self.go(9, self.at(d, yn, l, 1), ym)
            self.go(10, self.at(d, yn, l), core)

        def pair(self):
            ref = self.at(d, y, 1 - l)
            self.got(0, ref)
            self.go(4, ref, yp)
            self.go(5, ref, ym)
            self.go(6, ref, core)

        def second_ring(self):
            self.got(4, self.at(d, yb, 1 - l))
            self.go(11, self.at(d, yb, 1 - l, 0), yp)
            self.go(12, self.at(d, yb, 1 - l), core)
            self.got(5, self.at(d, yn, 1 - l))
            self.go(13, self.at(d, yn, 1 - l, 1), ym)
            self.go(14, self.at(d, yn, 1 - l), core)

        def near(self):
            self.local.wait()
            self.got(3, self.at(1 - d, y, l))
            self.got(6, self.at(1 - d, y, 1 - l))
            self.got(8, self.at(1 - d, yb, l))
            self.got(10, self.at(1 - d, yn, l))
            self.got(12, self.at(1 - d, yb, 1 - l))
            self.got(14, self.at(1 - d, yn, 1 - l))

        def far(self):
            self.got(7, self.at(d, yf, l, 0))
            self.got(9, self.at(d, yf, l, 1))
            self.go(15, self.at(d, yf, l), core)
            self.got(11, self.at(d, yf, 1 - l, 0))
            self.got(13, self.at(d, yf, 1 - l, 1))
            self.go(16, self.at(d, yf, 1 - l), core)

        def rest(self):
            self.got(15, self.at(1 - d, yf, l))
            self.got(16, self.at(1 - d, yf, 1 - l))

    wqkv = Weight(wq, G, 384, ls.at[0])
    wout = Weight(wo, woG, 192, ls.at[1])
    wqkv.own()

    seg_id = net.ids(1)[0]
    net.send(seg_id, segb.at[0], segb.at[1], core)
    st_ids = net.ids(7)
    for k in range(1, 8):
        net.send(st_ids[k - 1], st.at[c], st.at[c], col_peers[k - 1])
    for k in range(1, 8):
        net.recv(st_ids[k - 1], st.at[(c + 8 - k) % 8], core)
    means = [st[k, 0:1, :] for k in range(8)]
    mean = sum(means) * 0.125
    total_sq = sum(st[k, 1:2, :] for k in range(8))
    total_sq = total_sq + 768.0 * sum((m - mean) * (m - mean) for m in means)
    inv = lax.rsqrt(total_sq * (1.0 / 6144.0) + EPS)
    sub = lax.broadcasted_iota(jnp.int32, (128, 512), 0)
    columns = jnp.where(sub == 0, mean, jnp.where(sub == 1, inv, 0.0)).T
    lanes = pl.ds(pl.multiple_of(c * 768, 768), 768)
    normed = (tok[...].astype(F32) - columns[:, 0:1]) * columns[:, 1:2]
    modulated = (normed * (1.0 + scale[0:1, lanes]) + shift[0:1, lanes]).astype(BF16)
    swap_ids = net.ids(2)
    halves = (pl.ds(0, 256), pl.ds(256, 256))

    def keep_x():
        Xg[c] = modulated

    def swap_x():
        mod[...] = modulated
        for p in range(2):
            net.send(swap_ids[p], mod.at[halves[p]], Xg.at[c, halves[p]], sw, keep=False)

    both_sides(keep_x, swap_x)

    net.recv(seg_id, segb.at[1], core)
    slot = jnp.where(d == l, 0, 1)
    lane_row = lax.broadcasted_iota(jnp.int32, (1, 128), 1).astype(F32)

    def fill(b, carry):
        code = segb[slot, pl.ds(b, 1), :]
        other = jnp.where(lane_row == code, 0.0, 1.0).astype(BF16)
        tile = jnp.broadcast_to(other, (128, 128))
        ones = jnp.ones((128, 128), BF16)
        rows = pl.ds(pl.multiple_of((b % 4) * 128, 128), 128)
        for j in range(3):
            kvx[j, b // 4, rows, 384:512] = tile
            kvx[j, b // 4, rows, 0:128] = ones
        return carry

    def fill_q(b, carry):
        code = segb[slot, pl.ds(4 * rr + b, 1), :]
        same = jnp.where(lane_row == code, -FAR, 0.0).astype(BF16)
        tile = jnp.broadcast_to(same, (128, 128))
        rows = pl.ds(pl.multiple_of(b * 128, 128), 128)
        for j in range(3):
            qx[j, rows, 128:256] = tile
        return carry

    def wait_swap_x():
        for p in range(2):
            net.recv(swap_ids[p], Xg.at[c, halves[p]], sw)

    pl.when(d != l)(wait_swap_x)

    xi = net.ids(14)

    def xat(hh, zz, p):
        return Xg.at[4 * hh + zz, halves[p]]

    def xgo(i, ref, device):
        net.send(xi[i], ref, ref, device)

    def xgot(i, ref):
        net.recv(xi[i], ref, core)

    xgo(2, xat(h, z, 0), zp)
    xgo(5, xat(h, z, 1), zm)
    xgo(0, xat(h, z, 0), xh)
    xgo(1, xat(h, z, 1), xh)
    xgo(3, xat(h, z, 1), zp)
    xgo(4, xat(h, z, 0), zm)

    lax.fori_loop(0, 32, fill, 0)
    lax.fori_loop(0, 4, fill_q, 0)

    wqkv.first_ring()
    xgot(2, xat(h, zb, 0))
    xgo(6, xat(h, zb, 0), zp)
    xgot(5, xat(h, zn, 1))
    xgo(7, xat(h, zn, 1), zm)
    wqkv.pair()
    xgot(0, xat(h2, z, 0))
    xgo(8, xat(h2, z, 0), zp)
    xgo(10, xat(h2, z, 0), zm)
    xgot(1, xat(h2, z, 1))
    xgo(11, xat(h2, z, 1), zm)
    xgo(9, xat(h2, z, 1), zp)
    wqkv.second_ring()
    xgot(8, xat(h2, zb, 0))
    xgo(12, xat(h2, zb, 0), zp)
    xgot(11, xat(h2, zn, 1))
    xgo(13, xat(h2, zn, 1), zm)

    a0 = yf
    delta = (zf + 4 - yf) % 4
    third = jnp.where(delta == 0, 1, delta)
    e0 = (a0 + jnp.where(third == 1, 2, 1)) % 4
    e1 = (a0 + jnp.where(third == 3, 2, 3)) % 4
    e2 = (a0 + third) % 4

    def product(block, j):
        left = Xg[block]
        cols = slice(384 * j, 384 * (j + 1))
        right = jnp.concatenate([G[2 * block, :, cols], G[2 * block + 1, :, cols]], axis=0)
        return jnp.dot(left, right, preferred_element_type=F32)

    acc[...] = jnp.zeros_like(acc)
    wqkv.near()
    for i, hh, zz, p in ((3, h, zb, 1), (4, h, zn, 0), (9, h2, zb, 1), (10, h2, zn, 0)):
        xgot(i, xat(hh, zz, p))

    def early(s, carry):
        block = 4 * (s % 2) + jnp.where(s < 2, e0, e1)
        for j in range(3):
            acc[j] += product(block, j)
        return carry

    lax.fori_loop(0, 4, early, 0)
    wqkv.far()
    wout.own()
    xgot(6, xat(h, zf, 0))
    xgot(7, xat(h, zf, 1))
    xgot(12, xat(h2, zf, 0))
    xgot(13, xat(h2, zf, 1))
    wqkv.rest()

    def rms(v):
        return v * lax.rsqrt(jnp.mean(v * v, axis=-1, keepdims=True) + EPS)

    def finish(j):
        def late(s, carry):
            block = 4 * (s % 2) + jnp.where(s < 2, e2, a0)
            acc[j] += product(block, j)
            return carry

        lax.fori_loop(0, 4, late, 0)
        qx[j, :, 0:128] = (rms(acc[j, :, 0:128]) * gain[j]).astype(BF16)
        kvx[j, rr, :, 256:384] = rms(acc[j, :, 128:256]).astype(BF16)
        kvx[j, rr, :, 128:256] = acc[j, :, 256:384].astype(BF16)

    ki = [net.ids(8) for _ in range(3)]

    def kat(j, yy, dd, p=None):
        rows = pl.ds(0, 512) if p is None else halves[p]
        return kvx.at[j, 2 * yy + dd, rows, pl.ds(128, 256)]

    def kgo(j, i, ref, device):
        net.send(ki[j][i], ref, ref, device)

    def kgot(j, i, ref):
        net.recv(ki[j][i], ref, core)

    def kv_own(j):
        me = kat(j, y, d)
        kgo(j, 0, me, yp)
        kgo(j, 1, me, ym)
        kgo(j, 2, me, core)

    def kv_forward(j):
        kgot(j, 0, kat(j, yb, d))
        kgo(j, 3, kat(j, yb, d, 0), yp)
        kgo(j, 4, kat(j, yb, d), core)
        kgot(j, 1, kat(j, yn, d))
        kgo(j, 5, kat(j, yn, d, 1), ym)
        kgo(j, 6, kat(j, yn, d), core)

    def kv_far(j):
        kgot(j, 3, kat(j, yf, d, 0))
        kgot(j, 5, kat(j, yf, d, 1))
        kgo(j, 7, kat(j, yf, d), core)

    power = (1.0 / HD**0.5) * math.log2(math.e)

    def attend(j, amount, row_of):
        def step(s, carry):
            key_row = row_of(s // 2)
            rows = pl.ds(pl.multiple_of((s % 2) * 256, 256), 256)

            @pl.when(jnp.abs(key_row - rr) <= 4)
            def _():
                scores = lax.dot_general(
                    qx[j, rows, :],
                    kvx[j, key_row, :, 256:512],
                    (((1,), (1,)), ((), ())),
                    preferred_element_type=F32,
                )
                weights = jnp.exp2(scores * power).astype(BF16)
                oacc[rows, :] += jnp.dot(
                    weights, kvx[j, key_row, :, 0:256], preferred_element_type=F32
                )

            return carry

        lax.fori_loop(0, 2 * amount, step, 0)

    def attend_here(j):
        oacc[...] = jnp.zeros_like(oacc)
        kgot(j, 2, kat(j, y, 1 - d))
        attend(j, 2, lambda k: 2 * y + k)

    def attend_near(j):
        kgot(j, 4, kat(j, yb, 1 - d))
        kgot(j, 6, kat(j, yn, 1 - d))
        attend(j, 4, lambda k: 2 * ((y + 3 + 2 * (k // 2)) % 4) + k % 2)

    def attend_far(j):
        kgot(j, 7, kat(j, yf, 1 - d))
        attend(j, 2, lambda k: 2 * yf + k)

    ai = [net.ids(10) for _ in range(3)]

    def aat(j, hh, zz, p=None):
        ref = attg.at[j, 4 * hh + zz]
        return ref if p is None else ref.at[halves[p]]

    def ago(j, i, ref, device):
        net.send(ai[j][i], ref, ref, device)

    def agot(j, i, ref):
        net.recv(ai[j][i], ref, core)

    def att_put(j):
        value = (oacc[:, 128:256] / oacc[:, 0:128]).astype(BF16)

        def keep():
            attg[j, c] = value

        def swap():
            ast[j] = value
            net.send(ai[j][9], ast.at[j], attg.at[j, c], sw, keep=False)

        both_sides(keep, swap)

    def att_own(j):
        pl.when(d != l)(lambda: net.recv(ai[j][9], attg.at[j, c], sw))
        me = aat(j, h, z)
        ago(j, 0, me, xh)
        ago(j, 1, me, zp)
        ago(j, 2, me, zm)

    def att_forward(j):
        agot(j, 1, aat(j, h, zb))
        ago(j, 3, aat(j, h, zb, 0), zp)
        agot(j, 2, aat(j, h, zn))
        ago(j, 4, aat(j, h, zn, 1), zm)
        agot(j, 0, aat(j, h2, z))
        ago(j, 5, aat(j, h2, z), zp)
        ago(j, 6, aat(j, h2, z), zm)

    def att_second(j):
        agot(j, 5, aat(j, h2, zb))
        ago(j, 7, aat(j, h2, zb, 0), zp)
        agot(j, 6, aat(j, h2, zn))
        ago(j, 8, aat(j, h2, zn, 1), zm)

    def att_rest(j):
        agot(j, 3, aat(j, h, zf, 0))
        agot(j, 4, aat(j, h, zf, 1))
        agot(j, 7, aat(j, h2, zf, 0))
        agot(j, 8, aat(j, h2, zf, 1))

    def wrows(block, j):
        pieces = []
        for e in range(2):
            unit = 6 * block + 2 * j + e
            pieces.append(woG[unit // 3, pl.ds(pl.multiple_of((unit % 3) * 64, 64), 64), :])
        return pieces

    def project_out(j):
        def step(p, carry):
            left = jnp.concatenate([attg[j, 2 * p], attg[j, 2 * p + 1]], axis=1)
            right = jnp.concatenate(wrows(2 * p, j) + wrows(2 * p + 1, j), axis=0)
            bacc[...] += jnp.dot(left, right, preferred_element_type=F32)
            return carry

        lax.fori_loop(0, 4, step, 0)

    finish(0)
    kv_own(0)
    finish(1)
    finish(2)
    attend_here(0)
    kv_forward(0)
    kv_own(1)
    attend_near(0)
    kv_far(0)
    attend_far(0)
    att_put(0)
    kv_forward(1)
    kv_own(2)
    att_own(0)
    attend_here(1)
    attend_near(1)
    att_forward(0)
    kv_far(1)
    attend_far(1)
    att_put(1)
    kv_forward(2)
    att_own(1)
    att_second(0)
    wout.pair()
    wout.first_ring()
    attend_here(2)
    attend_near(2)
    kv_far(2)
    att_forward(1)
    attend_far(2)
    att_put(2)
    att_own(2)
    wout.second_ring()
    att_second(1)
    bacc[...] = jnp.zeros_like(bacc)
    att_forward(2)
    wout.far()
    att_rest(0)
    wout.near()
    wout.rest()
    project_out(0)
    att_second(2)
    att_rest(1)
    project_out(1)
    att_rest(2)
    project_out(2)
    out[...] = (gate[...] * bacc[...]).astype(BF16)

    for copy in net.sent:
        copy.wait_send()

    @pl.when(d != l)
    def _():
        for p in range(2):
            net.copy(swap_ids[p], mod.at[halves[p]], Xg.at[c, halves[p]], sw).wait_send()
        for j in range(3):
            net.copy(ai[j][9], ast.at[j], attg.at[j, c], sw).wait_send()


def local(tokens, w_qkv, w_out, ada_shift, ada_scale, out_gate, head_gain, block_segment):
    vmem = pl.BlockSpec(memory_space=pltpu.VMEM)
    smem = pl.BlockSpec(memory_space=pltpu.SMEM)
    return pl.pallas_call(
        kernel,
        out_shape=jax.ShapeDtypeStruct((512, 768), BF16),
        in_specs=[vmem] * 6 + [smem] * 2,
        out_specs=vmem,
        scratch_shapes=[
            pltpu.VMEM((16, 384, 1152), BF16),
            pltpu.VMEM((8, 512, 768), BF16),
            pltpu.VMEM((3, 8, 512, 512), BF16),
            pltpu.VMEM((3, 512, 256), BF16),
            pltpu.VMEM((16, 192, 768), BF16),
            pltpu.VMEM((3, 8, 512, 128), BF16),
            pltpu.VMEM((3, 512, 384), F32),
            pltpu.VMEM((512, 256), F32),
            pltpu.VMEM((512, 768), F32),
            pltpu.VMEM((512, 768), BF16),
            pltpu.VMEM((3, 512, 128), BF16),
            pltpu.VMEM((8, 8, 512), F32),
            pltpu.VMEM((2, 32, 128), F32),
            pltpu.SemaphoreType.DMA((N_FLOWS,)),
            pltpu.SemaphoreType.DMA((N_FLOWS,)),
            pltpu.SemaphoreType.DMA((2,)),
        ],
        compiler_params=pltpu.CompilerParams(
            collective_id=0, has_side_effects=True, vmem_limit_bytes=60 * 2**20
        ),
    )(tokens, w_qkv, w_out, ada_shift, ada_scale, out_gate, head_gain, block_segment)


def solution(mesh):
    placed = (
        P(("dp", "row"), "col"),
        P(("dp", "row"), "col"),
        P(("dp", "row"), "col"),
        P("dp", None),
        P("dp", None),
        P("dp", "col"),
        P("col"),
        P("dp", None),
    )
    return jax.shard_map(
        local, mesh=mesh, in_specs=placed, out_specs=P(("dp", "row"), "col"), check_vma=False
    )
```

```python
import math

import jax
import jax.numpy as jnp
from jax import lax
from jax.experimental import pallas as pl
from jax.experimental.pallas import tpu as pltpu
from jax.sharding import PartitionSpec as P

HD = 128
BLK = 128
EPS = 1e-06
FAR = 2048.0
F32 = jnp.float32
BF16 = jnp.bfloat16
MESH = pl.DeviceIdType.MESH
N_FLOWS = 136


class Net:
    def __init__(self, ss, rs):
        self.ss, self.rs, self.count, self.sent = ss, rs, 0, []

    def ids(self, amount):
        first = self.count
        self.count += amount
        assert self.count <= N_FLOWS
        return list(range(first, self.count))

    def copy(self, i, src, dst, device):
        return pltpu.make_async_remote_copy(
            src_ref=src,
            dst_ref=dst,
            send_sem=self.ss.at[i],
            recv_sem=self.rs.at[i],
            device_id=device,
            device_id_type=MESH,
        )

    def send(self, i, src, dst, device, keep=True):
        copy = self.copy(i, src, dst, device)
        copy.start()
        if keep:
            self.sent.append(copy)
        return copy

    def add(self, i, src, dst, device):
        self.sent.append(self.copy(i, src, dst, device))

    def recv(self, i, ref, device):
        self.copy(i, ref, ref, device).wait_recv()


def kernel(
    tok_hbm, wq, wo, shift, scale, gate, gain, seg, out,
    tok, G, Xg, kvx, qx, woG, attg, acc, oacc, bacc, mod, ast, st, segb, ss, rs, ls,
):
    d, row, c = lax.axis_index("dp"), lax.axis_index("row"), lax.axis_index("col")
    y, l = row // 2, row % 2
    h, z = c // 4, c % 4
    yn, yf, yb = (y + 1) % 4, (y + 2) % 4, (y + 3) % 4
    zn, zf, zb = (z + 1) % 4, (z + 2) % 4, (z + 3) % 4
    h2 = 1 - h
    core = (1 - d, row, c)
    xl = (d, 2 * y + 1 - l, c)
    yp, ym = (d, 2 * yn + l, c), (d, 2 * yb + l, c)
    zp, zm = (d, row, 4 * h + zn), (d, row, 4 * h + zb)
    xh = (d, row, 4 * h2 + z)
    sw = (l, 2 * y + d, c)
    rr = 2 * y + d
    net = Net(ss, rs)

    def both_sides(first, second):
        pl.when(d == l)(first)
        pl.when(d != l)(second)

    barrier = pltpu.get_barrier_semaphore()
    col_peers = [(d, row, (c + k) % 8) for k in range(1, 8)]
    for peer in col_peers + [core, xl, yp, ym]:
        pl.semaphore_signal(barrier, inc=1, device_id=peer, device_id_type=MESH)

    @pl.when(d != l)
    def _():
        pl.semaphore_signal(barrier, inc=1, device_id=sw, device_id_type=MESH)

    tok_copy = pltpu.make_async_copy(tok_hbm, tok, ls.at[2])
    tok_copy.start()
    pl.semaphore_wait(barrier, 11 + (d + l) % 2)

    def wid(dd, yy, ll):
        return 8 * dd + 2 * yy + ll

    class Weight:
        def __init__(self, src, dst, rows, local_sem):
            self.src, self.dst, self.half = src, dst, rows // 2
            self.f = net.ids(17)
            self.local = pltpu.make_async_copy(src, dst.at[wid(d, y, l)], local_sem)

        def at(self, dd, yy, ll, part=None):
            ref = self.dst.at[wid(dd, yy, ll)]
            if part is None:
                return ref
            return ref.at[pl.ds(part * self.half, self.half)]

        def go(self, i, ref, device):
            net.send(self.f[i], ref, ref, device)

        def got(self, i, ref):
            net.recv(self.f[i], ref, core)

        def own(self):
            me = self.at(d, y, l)
            for i, device in ((1, yp), (2, ym), (0, xl), (3, core)):
                net.send(self.f[i], self.src, me, device)
            self.local.start()

        def first_ring(self):
            self.got(1, self.at(d, yb, l))
            self.go(7, self.at(d, yb, l, 0), yp)
            self.go(8, self.at(d, yb, l), core)
            self.got(2, self.at(d, yn, l))
            self.go(9, self.at(d, yn, l, 1), ym)
            self.go(10, self.at(d, yn, l), core)

        def pair(self):
            ref = self.at(d, y, 1 - l)
            self.got(0, ref)
            send_xh()
            self.go(4, ref, yp)
            self.go(5, ref, ym)
            self.go(6, ref, core)

        def second_ring(self):
            self.got(4, self.at(d, yb, 1 - l))
            self.go(11, self.at(d, yb, 1 - l, 0), yp)
            self.go(12, self.at(d, yb, 1 - l), core)
            self.got(5, self.at(d, yn, 1 - l))
            self.go(13, self.at(d, yn, 1 - l, 1), ym)
            self.go(14, self.at(d, yn, 1 - l), core)

        def near(self):
            self.local.wait()
            self.got(3, self.at(1 - d, y, l))
            self.got(6, self.at(1 - d, y, 1 - l))
            self.got(8, self.at(1 - d, yb, l))
            self.got(10, self.at(1 - d, yn, l))
            self.got(12, self.at(1 - d, yb, 1 - l))
            self.got(14, self.at(1 - d, yn, 1 - l))

        def far(self):
            self.got(7, self.at(d, yf, l, 0))
            self.got(9, self.at(d, yf, l, 1))
            self.go(15, self.at(d, yf, l), core)
            self.got(11, self.at(d, yf, 1 - l, 0))
            self.got(13, self.at(d, yf, 1 - l, 1))
            self.go(16, self.at(d, yf, 1 - l), core)

        def rest(self):
            self.got(15, self.at(1 - d, yf, l))
            self.got(16, self.at(1 - d, yf, 1 - l))

    class LateWeight(Weight):
        def own(self):
            me = self.at(d, y, l)
            for i, device in ((1, yp), (2, ym), (0, xl), (3, core)):
                net.send(self.f[i], self.src, me, device)
            self.local.start()

        def first_ring(self):
            for i, yy, part, device in ((1, yb, 0, yp), (2, yn, 1, ym)):
                self.got(i, self.at(d, yy, l))
                self.go(3 + i, self.at(d, yy, l, part), device)
                self.go(5 + i, self.at(d, yy, l), xl)
                self.go(7 + i, self.at(d, yy, l), core)

        def second_ring(self):
            self.got(4, self.at(d, yf, l, 0))
            self.got(5, self.at(d, yf, l, 1))
            self.go(10, self.at(d, yf, l), xl)
            self.go(11, self.at(d, yf, l), core)

        def pair(self):
            for i, yy, j in ((0, y, 12), (6, yb, 13), (7, yn, 14)):
                self.got(i, self.at(d, yy, 1 - l))
                self.go(j, self.at(d, yy, 1 - l), core)

        def far(self):
            self.got(10, self.at(d, yf, 1 - l))
            self.go(15, self.at(d, yf, 1 - l), core)

        def rest(self):
            self.local.wait()
            for i, yy, ll in ((3, y, l), (8, yb, l), (9, yn, l), (11, yf, l)):
                self.got(i, self.at(1 - d, yy, ll))
            for i, yy in ((12, y), (13, yb), (14, yn), (15, yf)):
                self.got(i, self.at(1 - d, yy, 1 - l))

    wqkv = Weight(wq, G, 384, ls.at[0])
    wout = LateWeight(wo, woG, 192, ls.at[1])
    wqkv.own()
    tok_copy.wait()

    x = tok[...].astype(F32)
    part_mean = jnp.sum(x, axis=-1, keepdims=True) * (1.0 / 768.0)
    off = x - part_mean
    part_sq = jnp.sum(off * off, axis=-1, keepdims=True)
    lane = lax.broadcasted_iota(jnp.int32, (512, 128), 1)
    columns = jnp.where(lane == 0, part_mean, jnp.where(lane == 1, part_sq, 0.0))
    st[c] = columns.T[:8]
    for b in range(32):
        segb[0, b : b + 1, :] = jnp.full((1, 128), seg[0, b], jnp.int32).astype(F32)


    seg_id = net.ids(1)[0]
    net.send(seg_id, segb.at[0], segb.at[1], core)
    st_ids = net.ids(7)
    for k in range(1, 8):
        net.send(st_ids[k - 1], st.at[c], st.at[c], col_peers[k - 1])
    for k in range(1, 8):
        net.recv(st_ids[k - 1], st.at[(c + 8 - k) % 8], core)
    means = [st[k, 0:1, :] for k in range(8)]
    mean = sum(means) * 0.125
    total_sq = sum(st[k, 1:2, :] for k in range(8))
    total_sq = total_sq + 768.0 * sum((m - mean) * (m - mean) for m in means)
    inv = lax.rsqrt(total_sq * (1.0 / 6144.0) + EPS)
    sub = lax.broadcasted_iota(jnp.int32, (128, 512), 0)
    columns = jnp.where(sub == 0, mean, jnp.where(sub == 1, inv, 0.0)).T
    lanes = pl.ds(pl.multiple_of(c * 768, 768), 768)
    normed = (tok[...].astype(F32) - columns[:, 0:1]) * columns[:, 1:2]
    modulated = (normed * (1.0 + scale[0:1, lanes]) + shift[0:1, lanes]).astype(BF16)
    swap_ids = net.ids(2)
    halves = (pl.ds(0, 256), pl.ds(256, 256))

    def keep_x():
        Xg[c] = modulated

    def swap_x():
        mod[...] = modulated
        for p in range(2):
            net.send(swap_ids[p], mod.at[halves[p]], Xg.at[c, halves[p]], sw, keep=False)

    both_sides(keep_x, swap_x)

    net.recv(seg_id, segb.at[1], core)
    slot = jnp.where(d == l, 0, 1)
    lane_row = lax.broadcasted_iota(jnp.int32, (1, 128), 1).astype(F32)

    def fill(b, carry):
        code = segb[slot, pl.ds(b, 1), :]
        other = jnp.where(lane_row == code, 0.0, 1.0).astype(BF16)
        tile = jnp.broadcast_to(other, (128, 128))
        ones = jnp.ones((128, 128), BF16)
        rows = pl.ds(pl.multiple_of((b % 4) * 128, 128), 128)
        for j in range(3):
            kvx[j, b // 4, rows, 384:512] = tile
            kvx[j, b // 4, rows, 0:128] = ones
        return carry

    def fill_q(b, carry):
        code = segb[slot, pl.ds(4 * rr + b, 1), :]
        same = jnp.where(lane_row == code, -FAR, 0.0).astype(BF16)
        tile = jnp.broadcast_to(same, (128, 128))
        rows = pl.ds(pl.multiple_of(b * 128, 128), 128)
        for j in range(3):
            qx[j, rows, 128:256] = tile
        return carry

    def wait_swap_x():
        for p in range(2):
            net.recv(swap_ids[p], Xg.at[c, halves[p]], sw)

    pl.when(d != l)(wait_swap_x)

    xi = net.ids(14)

    def xat(hh, zz, p):
        return Xg.at[4 * hh + zz, halves[p]]

    def xgo(i, ref, device, keep=True):
        net.send(xi[i], ref, ref, device, keep)

    def xgot(i, ref):
        net.recv(xi[i], ref, core)

    def send_xh():
        xgo(0, xat(h, z, 0), xh)
        xgo(1, xat(h, z, 1), xh)

    xgo(2, xat(h, z, 0), zp)
    xgo(5, xat(h, z, 1), zm)
    xgo(3, xat(h, z, 1), zp)
    xgo(4, xat(h, z, 0), zm)

    lax.fori_loop(0, 32, fill, 0)
    lax.fori_loop(0, 4, fill_q, 0)

    def x_forward():
        xgot(2, xat(h, zb, 0))
        xgo(6, xat(h, zb, 0), zp, None)
        xgot(5, xat(h, zn, 1))
        xgo(7, xat(h, zn, 1), zm, None)

    pl.when(d == l)(x_forward)
    wqkv.first_ring()
    wqkv.pair()
    pl.when(d != l)(x_forward)
    net.add(xi[6], xat(h, zb, 0), xat(h, zb, 0), zp)
    net.add(xi[7], xat(h, zn, 1), xat(h, zn, 1), zm)
    xgot(0, xat(h2, z, 0))
    xgo(8, xat(h2, z, 0), zp)
    xgo(10, xat(h2, z, 0), zm)
    xgot(1, xat(h2, z, 1))
    xgo(11, xat(h2, z, 1), zm)
    xgo(9, xat(h2, z, 1), zp)
    wqkv.second_ring()
    xgot(8, xat(h2, zb, 0))
    xgo(12, xat(h2, zb, 0), zp)
    xgot(11, xat(h2, zn, 1))
    xgo(13, xat(h2, zn, 1), zm)

    a0 = yf
    delta = (zf + 4 - yf) % 4
    third = jnp.where(delta == 0, 1, delta)
    e0 = (a0 + jnp.where(third == 1, 2, 1)) % 4
    e1 = (a0 + jnp.where(third == 3, 2, 3)) % 4
    e2 = (a0 + third) % 4

    def product(block, j):
        left = Xg[block]
        cols = slice(384 * j, 384 * (j + 1))
        right = jnp.concatenate([G[2 * block, :, cols], G[2 * block + 1, :, cols]], axis=0)
        return jnp.dot(left, right, preferred_element_type=F32)

    acc[...] = jnp.zeros_like(acc)
    wqkv.near()
    for i, hh, zz, p in ((3, h, zb, 1), (4, h, zn, 0), (9, h2, zb, 1), (10, h2, zn, 0)):
        xgot(i, xat(hh, zz, p))

    def early(s, carry):
        block = 4 * (s % 2) + jnp.where(s < 2, e0, e1)
        for j in range(3):
            acc[j] += product(block, j)
        return carry

    lax.fori_loop(0, 4, early, 0)
    wqkv.far()
    wout.own()
    xgot(6, xat(h, zf, 0))
    xgot(7, xat(h, zf, 1))
    xgot(12, xat(h2, zf, 0))
    xgot(13, xat(h2, zf, 1))
    wqkv.rest()

    def rms(v):
        return v * lax.rsqrt(jnp.mean(v * v, axis=-1, keepdims=True) + EPS)

    def finish(j):
        def late(s, carry):
            block = 4 * (s % 2) + jnp.where(s < 2, e2, a0)
            acc[j] += product(block, j)
            return carry

        lax.fori_loop(0, 4, late, 0)
        qx[j, :, 0:128] = (rms(acc[j, :, 0:128]) * gain[j]).astype(BF16)
        kvx[j, rr, :, 256:384] = rms(acc[j, :, 128:256]).astype(BF16)
        kvx[j, rr, :, 128:256] = acc[j, :, 256:384].astype(BF16)

    ki = [net.ids(8) for _ in range(3)]

    def kat(j, yy, dd, p=None):
        rows = pl.ds(0, 512) if p is None else halves[p]
        return kvx.at[j, 2 * yy + dd, rows, pl.ds(128, 256)]

    def kgo(j, i, ref, device):
        net.send(ki[j][i], ref, ref, device)

    def kgot(j, i, ref):
        net.recv(ki[j][i], ref, core)

    def kv_own(j):
        me = kat(j, y, d)
        kgo(j, 0, me, yp)
        kgo(j, 1, me, ym)
        kgo(j, 2, me, core)

    def kv_forward(j):
        kgot(j, 0, kat(j, yb, d))
        kgo(j, 3, kat(j, yb, d, 0), yp)
        kgo(j, 4, kat(j, yb, d), core)
        kgot(j, 1, kat(j, yn, d))
        kgo(j, 5, kat(j, yn, d, 1), ym)
        kgo(j, 6, kat(j, yn, d), core)

    def kv_far(j):
        kgot(j, 3, kat(j, yf, d, 0))
        kgot(j, 5, kat(j, yf, d, 1))
        kgo(j, 7, kat(j, yf, d), core)

    power = (1.0 / HD**0.5) * math.log2(math.e)

    def attend(j, amount, row_of):
        def step(s, carry):
            key_row = row_of(s // 2)
            rows = pl.ds(pl.multiple_of((s % 2) * 256, 256), 256)

            @pl.when(jnp.abs(key_row - rr) <= 4)
            def _():
                scores = lax.dot_general(
                    qx[j, rows, :],
                    kvx[j, key_row, :, 256:512],
                    (((1,), (1,)), ((), ())),
                    preferred_element_type=F32,
                )
                weights = jnp.exp2(scores * power).astype(BF16)
                oacc[rows, :] += jnp.dot(
                    weights, kvx[j, key_row, :, 0:256], preferred_element_type=F32
                )

            return carry

        lax.fori_loop(0, 2 * amount, step, 0)

    def attend_here(j):
        oacc[...] = jnp.zeros_like(oacc)
        kgot(j, 2, kat(j, y, 1 - d))
        attend(j, 2, lambda k: 2 * y + k)

    def attend_near(j):
        kgot(j, 4, kat(j, yb, 1 - d))
        kgot(j, 6, kat(j, yn, 1 - d))
        attend(j, 4, lambda k: 2 * ((y + 3 + 2 * (k // 2)) % 4) + k % 2)

    def attend_far(j):
        kgot(j, 7, kat(j, yf, 1 - d))
        attend(j, 2, lambda k: 2 * yf + k)

    ai = [net.ids(10) for _ in range(3)]

    def aat(j, hh, zz, p=None):
        ref = attg.at[j, 4 * hh + zz]
        return ref if p is None else ref.at[halves[p]]

    def ago(j, i, ref, device):
        net.send(ai[j][i], ref, ref, device)

    def agot(j, i, ref):
        net.recv(ai[j][i], ref, core)

    def att_put(j):
        value = (oacc[:, 128:256] / oacc[:, 0:128]).astype(BF16)

        def keep():
            attg[j, c] = value

        def swap():
            ast[j] = value
            net.send(ai[j][9], ast.at[j], attg.at[j, c], sw, keep=False)

        both_sides(keep, swap)

    def att_own(j):
        pl.when(d != l)(lambda: net.recv(ai[j][9], attg.at[j, c], sw))
        me = aat(j, h, z)
        ago(j, 0, me, xh)
        ago(j, 1, me, zp)
        ago(j, 2, me, zm)

    def att_forward(j):
        agot(j, 1, aat(j, h, zb))
        ago(j, 3, aat(j, h, zb, 0), zp)
        agot(j, 2, aat(j, h, zn))
        ago(j, 4, aat(j, h, zn, 1), zm)
        agot(j, 0, aat(j, h2, z))
        ago(j, 5, aat(j, h2, z), zp)
        ago(j, 6, aat(j, h2, z), zm)

    def att_second(j):
        agot(j, 5, aat(j, h2, zb))
        ago(j, 7, aat(j, h2, zb, 0), zp)
        agot(j, 6, aat(j, h2, zn))
        ago(j, 8, aat(j, h2, zn, 1), zm)

    def att_rest(j):
        agot(j, 3, aat(j, h, zf, 0))
        agot(j, 4, aat(j, h, zf, 1))
        agot(j, 7, aat(j, h2, zf, 0))
        agot(j, 8, aat(j, h2, zf, 1))

    def wrows(block, j):
        pieces = []
        for e in range(2):
            unit = 6 * block + 2 * j + e
            pieces.append(woG[unit // 3, pl.ds(pl.multiple_of((unit % 3) * 64, 64), 64), :])
        return pieces

    def project_out(j):
        def step(p, carry):
            left = jnp.concatenate([attg[j, 2 * p], attg[j, 2 * p + 1]], axis=1)
            right = jnp.concatenate(wrows(2 * p, j) + wrows(2 * p + 1, j), axis=0)
            bacc[...] += jnp.dot(left, right, preferred_element_type=F32)
            return carry

        lax.fori_loop(0, 4, step, 0)

    finish(0)
    kv_own(0)
    wout.first_ring()
    finish(1)
    finish(2)
    wout.second_ring()
    attend_here(0)
    kv_forward(0)
    kv_own(1)
    attend_near(0)
    kv_far(0)
    wout.pair()
    attend_far(0)
    att_put(0)
    kv_forward(1)
    kv_own(2)
    att_own(0)
    attend_here(1)
    attend_near(1)
    att_forward(0)
    kv_far(1)
    attend_far(1)
    att_put(1)
    kv_forward(2)
    att_own(1)
    att_second(0)
    wout.far()
    attend_here(2)
    attend_near(2)
    kv_far(2)
    att_forward(1)
    attend_far(2)
    att_put(2)
    att_own(2)
    att_second(1)
    bacc[...] = jnp.zeros_like(bacc)
    att_rest(0)
    wout.rest()
    project_out(0)
    att_forward(2)
    att_rest(1)
    project_out(1)
    att_second(2)
    att_rest(2)
    project_out(2)
    out[...] = (gate[...] * bacc[...]).astype(BF16)

    for copy in net.sent:
        copy.wait_send()

    @pl.when(d != l)
    def _():
        for p in range(2):
            net.copy(swap_ids[p], mod.at[halves[p]], Xg.at[c, halves[p]], sw).wait_send()
        for j in range(3):
            net.copy(ai[j][9], ast.at[j], attg.at[j, c], sw).wait_send()


def local(tokens, w_qkv, w_out, ada_shift, ada_scale, out_gate, head_gain, block_segment):
    vmem = pl.BlockSpec(memory_space=pltpu.VMEM)
    smem = pl.BlockSpec(memory_space=pltpu.SMEM)
    anyw = pl.BlockSpec(memory_space=pl.ANY)
    return pl.pallas_call(
        kernel,
        out_shape=jax.ShapeDtypeStruct((512, 768), BF16),
        in_specs=[anyw] * 3 + [vmem] * 3 + [smem] * 2,
        out_specs=vmem,
        scratch_shapes=[
            pltpu.VMEM((512, 768), BF16),
            pltpu.VMEM((16, 384, 1152), BF16),
            pltpu.VMEM((8, 512, 768), BF16),
            pltpu.VMEM((3, 8, 512, 512), BF16),
            pltpu.VMEM((3, 512, 256), BF16),
            pltpu.VMEM((16, 192, 768), BF16),
            pltpu.VMEM((3, 8, 512, 128), BF16),
            pltpu.VMEM((3, 512, 384), F32),
            pltpu.VMEM((512, 256), F32),
            pltpu.VMEM((512, 768), F32),
            pltpu.VMEM((512, 768), BF16),
            pltpu.VMEM((3, 512, 128), BF16),
            pltpu.VMEM((8, 8, 512), F32),
            pltpu.VMEM((2, 32, 128), F32),
            pltpu.SemaphoreType.DMA((N_FLOWS,)),
            pltpu.SemaphoreType.DMA((N_FLOWS,)),
            pltpu.SemaphoreType.DMA((3,)),
        ],
        compiler_params=pltpu.CompilerParams(
            collective_id=0, has_side_effects=True, vmem_limit_bytes=60 * 2**20
        ),
    )(tokens, w_qkv, w_out, ada_shift, ada_scale, out_gate, head_gain, block_segment)


def solution(mesh):
    placed = (
        P(("dp", "row"), "col"),
        P(("dp", "row"), "col"),
        P(("dp", "row"), "col"),
        P("dp", None),
        P("dp", None),
        P("dp", "col"),
        P("col"),
        P("dp", None),
    )
    return jax.shard_map(
        local, mesh=mesh, in_specs=placed, out_specs=P(("dp", "row"), "col"), check_vma=False
    )
```

```python
import math

import jax
import jax.numpy as jnp
from jax import lax
from jax.experimental import pallas as pl
from jax.experimental.pallas import tpu as pltpu
from jax.sharding import PartitionSpec as P

HD = 128
BLK = 128
EPS = 1e-06
FAR = 2048.0
F32 = jnp.float32
BF16 = jnp.bfloat16
MESH = pl.DeviceIdType.MESH
N_FLOWS = 128


class Net:
    def __init__(self, ss, rs):
        self.ss, self.rs, self.count, self.sent = ss, rs, 0, {}

    def ids(self, amount):
        first = self.count
        self.count += amount
        assert self.count <= N_FLOWS
        return list(range(first, self.count))

    def copy(self, i, src, dst, device):
        return pltpu.make_async_remote_copy(
            src_ref=src,
            dst_ref=dst,
            send_sem=self.ss.at[i],
            recv_sem=self.rs.at[i],
            device_id=device,
            device_id_type=MESH,
        )

    def send(self, i, src, dst, device, like, some=False):
        self.copy(i, src, dst, device).start()
        self.sent[i] = (like, some)

    def recv(self, i, ref, device):
        self.copy(i, ref, ref, device).wait_recv()


def kernel(
    tok_hbm, wq, wo, shift, scale, gate, gain, seg, out,
    tok, G, Xg, kvx, qx, woG, attg, acc, oacc, bacc, mod, ast, st, segb, ss, rs, ls,
):
    d, row, c = lax.axis_index("dp"), lax.axis_index("row"), lax.axis_index("col")
    y, l = row // 2, row % 2
    h, z = c // 4, c % 4
    yn, yf, yb = (y + 1) % 4, (y + 2) % 4, (y + 3) % 4
    zn, zf, zb = (z + 1) % 4, (z + 2) % 4, (z + 3) % 4
    h2 = 1 - h
    core = (1 - d, row, c)
    xl = (d, 2 * y + 1 - l, c)
    yp, ym = (d, 2 * yn + l, c), (d, 2 * yb + l, c)
    zp, zm = (d, row, 4 * h + zn), (d, row, 4 * h + zb)
    xh = (d, row, 4 * h2 + z)
    sw = (l, 2 * y + d, c)
    rr = 2 * y + d
    net = Net(ss, rs)

    def both_sides(first, second):
        pl.when(d == l)(first)
        pl.when(d != l)(second)

    tok_copy = pltpu.make_async_copy(tok_hbm, tok, ls.at[2])
    tok_copy.start()

    barrier = pltpu.get_barrier_semaphore()
    col_peers = [(d, row, (c + k) % 8) for k in range(1, 8)]
    for peer in col_peers + [core, xl, yp, ym]:
        pl.semaphore_signal(barrier, inc=1, device_id=peer, device_id_type=MESH)

    @pl.when(d != l)
    def _():
        pl.semaphore_signal(barrier, inc=1, device_id=sw, device_id_type=MESH)

    for b in range(32):
        segb[0, b : b + 1, :] = jnp.full((1, 128), seg[0, b], jnp.int32).astype(F32)

    tok_copy.wait()
    x = tok[...].astype(F32)
    part_mean = jnp.sum(x, axis=-1, keepdims=True) * (1.0 / 768.0)
    off = x - part_mean
    part_sq = jnp.sum(off * off, axis=-1, keepdims=True)
    lane = lax.broadcasted_iota(jnp.int32, (512, 128), 1)
    columns = jnp.where(lane == 0, part_mean, jnp.where(lane == 1, part_sq, 0.0))
    st[c] = columns.T[:8]
    pl.semaphore_wait(barrier, 11 + (d + l) % 2)

    def wid(dd, yy, ll):
        return 8 * dd + 2 * yy + ll

    class Weight:
        def __init__(self, src, dst, rows, local_sem):
            self.src, self.dst, self.half = src, dst, rows // 2
            self.parts = {None: pl.ds(0, rows), 0: pl.ds(0, rows // 2), 1: pl.ds(rows // 2, rows // 2)}
            self.f = dict(zip(self.names, net.ids(len(self.names))))
            self.local = pltpu.make_async_copy(src, dst.at[wid(d, y, l)], local_sem)

        names = (
            "own_yp0", "own_yp1", "own_ym0", "own_ym1", "own_xl0", "own_xl1",
            "own_core", "fwd_yp", "fwd_ym", "core_yb", "core_yn", "pair_yp0",
            "pair_yp1", "pair_ym0", "pair_ym1", "core_pair", "last_yp", "last_ym",
            "core_yb2", "core_yn2", "far0", "far1", "far2", "far3",
        )

        def at(self, dd, yy, ll, part=None):
            return self.dst.at[wid(dd, yy, ll), self.parts[part]]

        def go(self, name, device, dd, yy, ll, part=None, src=None):
            ref = self.at(dd, yy, ll, part)
            like = lambda: self.dst.at[0, self.parts[part]]
            net.send(self.f[name], ref if src is None else src, ref, device, like)

        def got(self, name, dd, yy, ll, part=None):
            net.recv(self.f[name], self.at(dd, yy, ll, part), core)

        def own(self, name, device, part=None):
            self.go(name, device, d, y, l, part, self.src.at[self.parts[part]])

        def own_y(self):
            self.own("own_yp0", yp, 0)
            self.own("own_ym1", ym, 1)
            self.own("own_yp1", yp, 1)
            self.own("own_ym0", ym, 0)

        def own_core(self):
            self.own("own_core", core)
            self.local.start()

        def own_x(self):
            self.own("own_xl0", xl, 0)
            self.own("own_xl1", xl, 1)

        def forward(self):
            self.got("own_yp0", d, yb, l, 0)
            self.go("fwd_yp", yp, d, yb, l, 0)
            self.got("own_ym1", d, yn, l, 1)
            self.go("fwd_ym", ym, d, yn, l, 1)

        def to_core(self):
            self.got("own_yp1", d, yb, l, 1)
            self.go("core_yb", core, d, yb, l)
            self.got("own_ym0", d, yn, l, 0)
            self.go("core_yn", core, d, yn, l)

        def pair(self):
            for p in range(2):
                self.got(f"own_xl{p}", d, y, 1 - l, p)
                self.go(f"pair_yp{p}", yp, d, y, 1 - l, p)
                self.go(f"pair_ym{p}", ym, d, y, 1 - l, p)
            self.go("core_pair", core, d, y, 1 - l)

        def forward_pair(self):
            self.got("pair_yp0", d, yb, 1 - l, 0)
            self.go("last_yp", yp, d, yb, 1 - l, 0)
            self.got("pair_ym1", d, yn, 1 - l, 1)
            self.go("last_ym", ym, d, yn, 1 - l, 1)

        def pair_to_core(self):
            self.got("pair_yp1", d, yb, 1 - l, 1)
            self.go("core_yb2", core, d, yb, 1 - l)
            self.got("pair_ym0", d, yn, 1 - l, 0)
            self.go("core_yn2", core, d, yn, 1 - l)

        def far(self):
            self.got("fwd_yp", d, yf, l, 0)
            self.go("far0", core, d, yf, l, 0)
            self.got("fwd_ym", d, yf, l, 1)
            self.go("far1", core, d, yf, l, 1)

        def far_pair(self):
            self.got("last_yp", d, yf, 1 - l, 0)
            self.go("far2", core, d, yf, 1 - l, 0)
            self.got("last_ym", d, yf, 1 - l, 1)
            self.go("far3", core, d, yf, 1 - l, 1)

        def near(self):
            self.local.wait()
            self.got("own_core", 1 - d, y, l)
            self.got("core_yb", 1 - d, yb, l)
            self.got("core_yn", 1 - d, yn, l)
            self.got("core_pair", 1 - d, y, 1 - l)
            self.got("core_yb2", 1 - d, yb, 1 - l)
            self.got("core_yn2", 1 - d, yn, 1 - l)

        def rest(self):
            for p in range(2):
                self.got(f"far{p}", 1 - d, yf, l, p)
                self.got(f"far{2 + p}", 1 - d, yf, 1 - l, p)

    wqkv = Weight(wq, G, 384, ls.at[0])
    wout = Weight(wo, woG, 192, ls.at[1])

    st_ids = net.ids(7)
    for k in range(1, 8):
        net.send(st_ids[k - 1], st.at[c], st.at[c], col_peers[k - 1], lambda: st.at[0])
    seg_id = net.ids(1)[0]
    net.send(seg_id, segb.at[0], segb.at[1], core, lambda: segb.at[0])
    wqkv.own_y()
    pl.when(d == l)(wqkv.own_x)
    wqkv.own_core()
    for k in range(1, 8):
        net.recv(st_ids[k - 1], st.at[(c + 8 - k) % 8], core)
    means = [st[k, 0:1, :] for k in range(8)]
    mean = sum(means) * 0.125
    total_sq = sum(st[k, 1:2, :] for k in range(8))
    total_sq = total_sq + 768.0 * sum((m - mean) * (m - mean) for m in means)
    inv = lax.rsqrt(total_sq * (1.0 / 6144.0) + EPS)
    sub = lax.broadcasted_iota(jnp.int32, (128, 512), 0)
    columns = jnp.where(sub == 0, mean, jnp.where(sub == 1, inv, 0.0)).T
    lanes = pl.ds(pl.multiple_of(c * 768, 768), 768)
    normed = (tok[...].astype(F32) - columns[:, 0:1]) * columns[:, 1:2]
    modulated = (normed * (1.0 + scale[0:1, lanes]) + shift[0:1, lanes]).astype(BF16)
    mod[...] = modulated
    swap_ids = net.ids(2)
    halves = (pl.ds(0, 256), pl.ds(256, 256))

    xi = net.ids(14)

    def xat(hh, zz, p):
        return Xg.at[4 * hh + zz, halves[p]]

    def xgo(i, ref, device, p, src=None):
        net.send(xi[i], ref if src is None else src, ref, device, lambda: mod.at[halves[p]])

    def xgot(i, ref):
        net.recv(xi[i], ref, core)

    def x_own(src):
        for i, p, device in ((2, 0, zp), (5, 1, zm), (0, 0, xh), (3, 1, zp), (4, 0, zm), (1, 1, xh)):
            xgo(i, xat(h, z, p), device, p, src(p))

    def x_forward():
        xgot(2, xat(h, zb, 0))
        xgo(6, xat(h, zb, 0), zp, 0)
        xgot(5, xat(h, zn, 1))
        xgo(7, xat(h, zn, 1), zm, 1)

    def x_pair(p):
        i, a, b = ((0, 8, 10), (1, 9, 11))[p]
        xgot(i, xat(h2, z, p))
        xgo(a, xat(h2, z, p), zp, p)
        xgo(b, xat(h2, z, p), zm, p)

    def x_forward_pair():
        xgot(8, xat(h2, zb, 0))
        xgo(12, xat(h2, zb, 0), zp, 0)
        xgot(11, xat(h2, zn, 1))
        xgo(13, xat(h2, zn, 1), zm, 1)

    slot = jnp.where(d == l, 0, 1)
    lane_row = lax.broadcasted_iota(jnp.int32, (1, 128), 1).astype(F32)

    def fill(b, carry):
        code = segb[slot, pl.ds(b, 1), :]
        other = jnp.where(lane_row == code, 0.0, 1.0).astype(BF16)
        tile = jnp.broadcast_to(other, (128, 128))
        ones = jnp.ones((128, 128), BF16)
        rows = pl.ds(pl.multiple_of((b % 4) * 128, 128), 128)
        for j in range(3):
            kvx[j, b // 4, rows, 384:512] = tile
            kvx[j, b // 4, rows, 0:128] = ones
        return carry

    def fill_q(b, carry):
        code = segb[slot, pl.ds(4 * rr + b, 1), :]
        same = jnp.where(lane_row == code, -FAR, 0.0).astype(BF16)
        tile = jnp.broadcast_to(same, (128, 128))
        rows = pl.ds(pl.multiple_of(b * 128, 128), 128)
        for j in range(3):
            qx[j, rows, 128:256] = tile
        return carry

    def start_kept():
        x_own(lambda p: mod.at[halves[p]])
        Xg[c] = mod[...]

    def start_traded():
        for p in range(2):
            net.send(swap_ids[p], mod.at[halves[p]], Xg.at[c, halves[p]], sw, lambda p=p: mod.at[halves[p]], True)
        wqkv.own_x()

    both_sides(start_kept, start_traded)
    net.recv(seg_id, segb.at[1], core)
    lax.fori_loop(0, 32, fill, 0)
    lax.fori_loop(0, 4, fill_q, 0)
    wqkv.forward()

    def kept():
        x_forward()
        wqkv.to_core()
        x_pair(0)
        wqkv.far()
        x_pair(1)
        wqkv.pair()
        x_forward_pair()
        wqkv.forward_pair()
        wqkv.pair_to_core()

    def traded():
        wqkv.pair()
        for p in range(2):
            net.recv(swap_ids[p], Xg.at[c, halves[p]], sw)
        x_own(lambda p: None)
        wqkv.to_core()
        x_forward()
        wqkv.far()
        wqkv.forward_pair()
        wqkv.pair_to_core()
        x_pair(0)
        x_pair(1)
        x_forward_pair()

    both_sides(kept, traded)
    wout.own_y()
    wout.own_x()
    wout.own_core()

    a0 = yf
    delta = (zf + 4 - yf) % 4
    third = jnp.where(delta == 0, 1, delta)
    e0 = (a0 + jnp.where(third == 1, 2, 1)) % 4
    e1 = (a0 + jnp.where(third == 3, 2, 3)) % 4
    e2 = (a0 + third) % 4

    def product(block, j):
        left = Xg[block]
        cols = slice(384 * j, 384 * (j + 1))
        right = jnp.concatenate([G[2 * block, :, cols], G[2 * block + 1, :, cols]], axis=0)
        return jnp.dot(left, right, preferred_element_type=F32)

    acc[...] = jnp.zeros_like(acc)
    wqkv.near()
    for i, hh, zz, p in ((3, h, zb, 1), (4, h, zn, 0), (9, h2, zb, 1), (10, h2, zn, 0)):
        xgot(i, xat(hh, zz, p))

    def early(s, carry):
        block = 4 * (s % 2) + jnp.where(s < 2, e0, e1)
        for j in range(3):
            acc[j] += product(block, j)
        return carry

    lax.fori_loop(0, 4, early, 0)
    wqkv.far_pair()
    xgot(6, xat(h, zf, 0))
    xgot(7, xat(h, zf, 1))
    xgot(12, xat(h2, zf, 0))
    xgot(13, xat(h2, zf, 1))
    wqkv.rest()

    def rms(v):
        return v * lax.rsqrt(jnp.mean(v * v, axis=-1, keepdims=True) + EPS)

    def finish(j):
        def late(s, carry):
            block = 4 * (s % 2) + jnp.where(s < 2, e2, a0)
            acc[j] += product(block, j)
            return carry

        lax.fori_loop(0, 4, late, 0)
        kvx[j, rr, :, 256:384] = rms(acc[j, :, 128:256]).astype(BF16)
        kvx[j, rr, :, 128:256] = acc[j, :, 256:384].astype(BF16)

    def finish_query(j):
        qx[j, :, 0:128] = (rms(acc[j, :, 0:128]) * gain[j]).astype(BF16)

    ki = [net.ids(8) for _ in range(3)]

    def kat(j, yy, dd, p=None):
        rows = pl.ds(0, 512) if p is None else halves[p]
        return kvx.at[j, 2 * yy + dd, rows, pl.ds(128, 256)]

    def kgo(j, i, ref, device, p=None):
        like = lambda: kvx.at[0, 0, pl.ds(0, 512) if p is None else halves[p], pl.ds(128, 256)]
        net.send(ki[j][i], ref, ref, device, like)

    def kgot(j, i, ref):
        net.recv(ki[j][i], ref, core)

    def kv_own(j):
        me = kat(j, y, d)
        kgo(j, 0, me, yp)
        kgo(j, 1, me, ym)
        kgo(j, 2, me, core)

    def kv_forward(j):
        kgot(j, 0, kat(j, yb, d))
        kgo(j, 3, kat(j, yb, d, 0), yp, 0)
        kgo(j, 4, kat(j, yb, d), core)
        kgot(j, 1, kat(j, yn, d))
        kgo(j, 5, kat(j, yn, d, 1), ym, 1)
        kgo(j, 6, kat(j, yn, d), core)

    def kv_far(j):
        kgot(j, 3, kat(j, yf, d, 0))
        kgot(j, 5, kat(j, yf, d, 1))
        kgo(j, 7, kat(j, yf, d), core)

    power = (1.0 / HD**0.5) * math.log2(math.e)

    def attend(j, amount, row_of):
        def step(s, carry):
            key_row = row_of(s // 2)
            rows = pl.ds(pl.multiple_of((s % 2) * 256, 256), 256)

            @pl.when(jnp.abs(key_row - rr) <= 4)
            def _():
                scores = lax.dot_general(
                    qx[j, rows, :],
                    kvx[j, key_row, :, 256:512],
                    (((1,), (1,)), ((), ())),
                    preferred_element_type=F32,
                )
                weights = jnp.exp2(scores * power).astype(BF16)
                oacc[rows, :] += jnp.dot(
                    weights, kvx[j, key_row, :, 0:256], preferred_element_type=F32
                )

            return carry

        lax.fori_loop(0, 2 * amount, step, 0)

    def attend_here(j):
        oacc[...] = jnp.zeros_like(oacc)
        kgot(j, 2, kat(j, y, 1 - d))
        attend(j, 2, lambda k: 2 * y + k)

    def attend_near(j):
        kgot(j, 4, kat(j, yb, 1 - d))
        kgot(j, 6, kat(j, yn, 1 - d))
        attend(j, 4, lambda k: 2 * ((y + 3 + 2 * (k // 2)) % 4) + k % 2)

    def attend_far(j):
        kgot(j, 7, kat(j, yf, 1 - d))
        attend(j, 2, lambda k: 2 * yf + k)

    ai = [net.ids(10) for _ in range(3)]

    def aat(j, hh, zz, p=None):
        ref = attg.at[j, 4 * hh + zz]
        return ref if p is None else ref.at[halves[p]]

    def ago(j, i, ref, device, p=None):
        like = lambda: ast.at[0] if p is None else ast.at[0, halves[p]]
        net.send(ai[j][i], ref, ref, device, like)

    def agot(j, i, ref):
        net.recv(ai[j][i], ref, core)

    def att_put(j):
        value = (oacc[:, 128:256] / oacc[:, 0:128]).astype(BF16)

        def keep():
            attg[j, c] = value

        def swap():
            ast[j] = value
            net.send(ai[j][9], ast.at[j], attg.at[j, c], sw, lambda: ast.at[0], True)

        both_sides(keep, swap)

    def att_own(j):
        pl.when(d != l)(lambda: net.recv(ai[j][9], attg.at[j, c], sw))
        me = aat(j, h, z)
        ago(j, 0, me, xh)
        ago(j, 1, me, zp)
        ago(j, 2, me, zm)

    def att_forward(j):
        agot(j, 1, aat(j, h, zb))
        ago(j, 3, aat(j, h, zb, 0), zp, 0)
        agot(j, 2, aat(j, h, zn))
        ago(j, 4, aat(j, h, zn, 1), zm, 1)
        agot(j, 0, aat(j, h2, z))
        ago(j, 5, aat(j, h2, z), zp)
        ago(j, 6, aat(j, h2, z), zm)

    def att_second(j):
        agot(j, 5, aat(j, h2, zb))
        ago(j, 7, aat(j, h2, zb, 0), zp, 0)
        agot(j, 6, aat(j, h2, zn))
        ago(j, 8, aat(j, h2, zn, 1), zm, 1)

    def att_rest(j):
        agot(j, 3, aat(j, h, zf, 0))
        agot(j, 4, aat(j, h, zf, 1))
        agot(j, 7, aat(j, h2, zf, 0))
        agot(j, 8, aat(j, h2, zf, 1))

    def wrows(block, j):
        pieces = []
        for e in range(2):
            unit = 6 * block + 2 * j + e
            pieces.append(woG[unit // 3, pl.ds(pl.multiple_of((unit % 3) * 64, 64), 64), :])
        return pieces

    def project_out(j):
        def step(p, carry):
            left = jnp.concatenate([attg[j, 2 * p], attg[j, 2 * p + 1]], axis=1)
            right = jnp.concatenate(wrows(2 * p, j) + wrows(2 * p + 1, j), axis=0)
            bacc[...] += jnp.dot(left, right, preferred_element_type=F32)
            return carry

        lax.fori_loop(0, 4, step, 0)

    finish(0)
    kv_own(0)
    finish(1)
    kv_own(1)
    finish(2)
    for j in range(3):
        finish_query(j)
    attend_here(0)
    kv_forward(0)
    kv_own(2)
    attend_near(0)
    kv_far(0)
    kv_forward(1)
    attend_far(0)
    att_put(0)
    attend_here(1)
    att_own(0)
    attend_near(1)
    kv_forward(2)
    wout.pair()
    wout.forward()
    kv_far(1)
    att_forward(0)
    attend_far(1)
    att_put(1)
    attend_here(2)
    att_own(1)
    attend_near(2)
    kv_far(2)
    att_second(0)
    attend_far(2)
    att_put(2)
    att_forward(1)
    wout.to_core()
    wout.far()
    att_own(2)
    wout.forward_pair()
    wout.pair_to_core()
    bacc[...] = jnp.zeros_like(bacc)
    att_second(1)
    att_rest(0)
    att_forward(2)
    wout.far_pair()
    att_second(2)
    wout.near()
    wout.rest()
    project_out(0)
    att_rest(1)
    project_out(1)
    att_rest(2)
    project_out(2)
    out[...] = (gate[...] * bacc[...]).astype(BF16)

    for i, (like, some) in net.sent.items():
        if not some:
            net.copy(i, like(), like(), core).wait_send()

    @pl.when(d != l)
    def _():
        for i, (like, some) in net.sent.items():
            if some:
                net.copy(i, like(), like(), core).wait_send()


def local(tokens, w_qkv, w_out, ada_shift, ada_scale, out_gate, head_gain, block_segment):
    vmem = pl.BlockSpec(memory_space=pltpu.VMEM)
    smem = pl.BlockSpec(memory_space=pltpu.SMEM)
    anyw = pl.BlockSpec(memory_space=pl.ANY)
    return pl.pallas_call(
        kernel,
        out_shape=jax.ShapeDtypeStruct((512, 768), BF16),
        in_specs=[anyw] * 3 + [vmem] * 3 + [smem] * 2,
        out_specs=vmem,
        scratch_shapes=[
            pltpu.VMEM((512, 768), BF16),
            pltpu.VMEM((16, 384, 1152), BF16),
            pltpu.VMEM((8, 512, 768), BF16),
            pltpu.VMEM((3, 8, 512, 512), BF16),
            pltpu.VMEM((3, 512, 256), BF16),
            pltpu.VMEM((16, 192, 768), BF16),
            pltpu.VMEM((3, 8, 512, 128), BF16),
            pltpu.VMEM((3, 512, 384), F32),
            pltpu.VMEM((512, 256), F32),
            pltpu.VMEM((512, 768), F32),
            pltpu.VMEM((512, 768), BF16),
            pltpu.VMEM((3, 512, 128), BF16),
            pltpu.VMEM((8, 8, 512), F32),
            pltpu.VMEM((2, 32, 128), F32),
            pltpu.SemaphoreType.DMA((N_FLOWS,)),
            pltpu.SemaphoreType.DMA((N_FLOWS,)),
            pltpu.SemaphoreType.DMA((3,)),
        ],
        compiler_params=pltpu.CompilerParams(
            collective_id=0, has_side_effects=True, vmem_limit_bytes=60 * 2**20
        ),
    )(tokens, w_qkv, w_out, ada_shift, ada_scale, out_gate, head_gain, block_segment)


def solution(mesh):
    placed = (
        P(("dp", "row"), "col"),
        P(("dp", "row"), "col"),
        P(("dp", "row"), "col"),
        P("dp", None),
        P("dp", None),
        P("dp", "col"),
        P("col"),
        P("dp", None),
    )
    return jax.shard_map(
        local, mesh=mesh, in_specs=placed, out_specs=P(("dp", "row"), "col"), check_vma=False
    )
```

```python
import math

import jax
import jax.numpy as jnp
from jax import lax
from jax.experimental import pallas as pl
from jax.experimental.pallas import tpu as pltpu
from jax.sharding import PartitionSpec as P

HD = 128
BLK = 128
EPS = 1e-06
FAR = 256.0
F32 = jnp.float32
BF16 = jnp.bfloat16
MESH = pl.DeviceIdType.MESH
N_FLOWS = 128


class Net:
    def __init__(self, ss, rs):
        self.ss, self.rs, self.count, self.sent = ss, rs, 0, {}

    def ids(self, amount):
        first = self.count
        self.count += amount
        assert self.count <= N_FLOWS
        return list(range(first, self.count))

    def copy(self, i, src, dst, device):
        return pltpu.make_async_remote_copy(
            src_ref=src,
            dst_ref=dst,
            send_sem=self.ss.at[i],
            recv_sem=self.rs.at[i],
            device_id=device,
            device_id_type=MESH,
        )

    def send(self, i, src, dst, device, like, some=False):
        self.copy(i, src, dst, device).start()
        self.sent[i] = (like, some)

    def recv(self, i, ref, device):
        self.copy(i, ref, ref, device).wait_recv()


def kernel(
    tok_hbm, wq, wo, shift, scale, gate, gain, seg, out,
    tok, G, Xg, kvx, qx, woG, attg, acc, oacc, bacc, mod, ast, st, segb, ss, rs, ls,
):
    d, row, c = lax.axis_index("dp"), lax.axis_index("row"), lax.axis_index("col")
    y, l = row // 2, row % 2
    h, z = c // 4, c % 4
    yn, yf, yb = (y + 1) % 4, (y + 2) % 4, (y + 3) % 4
    zn, zf, zb = (z + 1) % 4, (z + 2) % 4, (z + 3) % 4
    h2 = 1 - h
    core = (1 - d, row, c)
    xl = (d, 2 * y + 1 - l, c)
    yp, ym = (d, 2 * yn + l, c), (d, 2 * yb + l, c)
    zp, zm = (d, row, 4 * h + zn), (d, row, 4 * h + zb)
    xh = (d, row, 4 * h2 + z)
    sw = (l, 2 * y + d, c)
    rr = 2 * y + d
    net = Net(ss, rs)

    def both_sides(first, second):
        pl.when(d == l)(first)
        pl.when(d != l)(second)

    tok_copy = pltpu.make_async_copy(tok_hbm, tok, ls.at[2])
    tok_copy.start()

    barrier = pltpu.get_barrier_semaphore()
    col_peers = [(d, row, (c + k) % 8) for k in range(1, 8)]
    for peer in col_peers + [core, xl, yp, ym]:
        pl.semaphore_signal(barrier, inc=1, device_id=peer, device_id_type=MESH)

    @pl.when(d != l)
    def _():
        pl.semaphore_signal(barrier, inc=1, device_id=sw, device_id_type=MESH)

    for b in range(32):
        segb[0, b : b + 1, :] = jnp.full((1, 128), seg[0, b], jnp.int32).astype(F32)

    tok_copy.wait()
    x = tok[...].astype(F32)
    part_mean = jnp.sum(x, axis=-1, keepdims=True) * (1.0 / 768.0)
    off = x - part_mean
    part_sq = jnp.sum(off * off, axis=-1, keepdims=True)
    lane = lax.broadcasted_iota(jnp.int32, (512, 128), 1)
    columns = jnp.where(lane == 0, part_mean, jnp.where(lane == 1, part_sq, 0.0))
    st[c] = columns.T[:8]
    pl.semaphore_wait(barrier, 11 + (d + l) % 2)

    def wid(dd, yy, ll):
        return 8 * dd + 2 * yy + ll

    class Weight:
        def __init__(self, src, dst, rows, local_sem):
            self.src, self.dst, self.half = src, dst, rows // 2
            self.parts = {None: pl.ds(0, rows), 0: pl.ds(0, rows // 2), 1: pl.ds(rows // 2, rows // 2)}
            self.f = dict(zip(self.names, net.ids(len(self.names))))
            self.local = pltpu.make_async_copy(src, dst.at[wid(d, y, l)], local_sem)

        names = (
            "own_yp0", "own_yp1", "own_ym0", "own_ym1", "own_xl0", "own_xl1",
            "own_core", "fwd_yp", "fwd_ym", "core_yb", "core_yn", "pair_yp0",
            "pair_yp1", "pair_ym0", "pair_ym1", "core_pair", "last_yp", "last_ym",
            "core_yb2", "core_yn2", "far0", "far1", "far2", "far3",
        )

        def at(self, dd, yy, ll, part=None):
            return self.dst.at[wid(dd, yy, ll), self.parts[part]]

        def go(self, name, device, dd, yy, ll, part=None, src=None):
            ref = self.at(dd, yy, ll, part)
            like = lambda: self.dst.at[0, self.parts[part]]
            net.send(self.f[name], ref if src is None else src, ref, device, like)

        def got(self, name, dd, yy, ll, part=None):
            net.recv(self.f[name], self.at(dd, yy, ll, part), core)

        def own(self, name, device, part=None):
            self.go(name, device, d, y, l, part, self.src.at[self.parts[part]])

        def own_y(self):
            self.own("own_yp0", yp, 0)
            self.own("own_ym1", ym, 1)
            self.own("own_yp1", yp, 1)
            self.own("own_ym0", ym, 0)

        def own_core(self):
            self.own("own_core", core)
            self.local.start()

        def own_x(self):
            self.own("own_xl0", xl, 0)
            self.own("own_xl1", xl, 1)

        def forward(self):
            self.got("own_yp0", d, yb, l, 0)
            self.go("fwd_yp", yp, d, yb, l, 0)
            self.got("own_ym1", d, yn, l, 1)
            self.go("fwd_ym", ym, d, yn, l, 1)

        def to_core(self):
            self.got("own_yp1", d, yb, l, 1)
            self.go("core_yb", core, d, yb, l)
            self.got("own_ym0", d, yn, l, 0)
            self.go("core_yn", core, d, yn, l)

        def pair(self):
            for p in range(2):
                self.got(f"own_xl{p}", d, y, 1 - l, p)
                self.go(f"pair_yp{p}", yp, d, y, 1 - l, p)
                self.go(f"pair_ym{p}", ym, d, y, 1 - l, p)
            self.go("core_pair", core, d, y, 1 - l)

        def forward_pair(self):
            self.got("pair_yp0", d, yb, 1 - l, 0)
            self.go("last_yp", yp, d, yb, 1 - l, 0)
            self.got("pair_ym1", d, yn, 1 - l, 1)
            self.go("last_ym", ym, d, yn, 1 - l, 1)

        def pair_to_core(self):
            self.got("pair_yp1", d, yb, 1 - l, 1)
            self.go("core_yb2", core, d, yb, 1 - l)
            self.got("pair_ym0", d, yn, 1 - l, 0)
            self.go("core_yn2", core, d, yn, 1 - l)

        def far(self):
            self.got("fwd_yp", d, yf, l, 0)
            self.go("far0", core, d, yf, l, 0)
            self.got("fwd_ym", d, yf, l, 1)
            self.go("far1", core, d, yf, l, 1)

        def far_pair(self):
            self.got("last_yp", d, yf, 1 - l, 0)
            self.go("far2", core, d, yf, 1 - l, 0)
            self.got("last_ym", d, yf, 1 - l, 1)
            self.go("far3", core, d, yf, 1 - l, 1)

        def near(self):
            self.local.wait()
            self.got("own_core", 1 - d, y, l)
            self.got("core_yb", 1 - d, yb, l)
            self.got("core_yn", 1 - d, yn, l)
            self.got("core_pair", 1 - d, y, 1 - l)
            self.got("core_yb2", 1 - d, yb, 1 - l)
            self.got("core_yn2", 1 - d, yn, 1 - l)

        def rest(self):
            for p in range(2):
                self.got(f"far{p}", 1 - d, yf, l, p)
                self.got(f"far{2 + p}", 1 - d, yf, 1 - l, p)

    wqkv = Weight(wq, G, 384, ls.at[0])
    wout = Weight(wo, woG, 192, ls.at[1])

    st_ids = net.ids(7)
    for k in range(1, 8):
        net.send(st_ids[k - 1], st.at[c], st.at[c], col_peers[k - 1], lambda: st.at[0])
    seg_id = net.ids(1)[0]
    net.send(seg_id, segb.at[0], segb.at[1], core, lambda: segb.at[0])
    wqkv.own_y()
    pl.when(d == l)(wqkv.own_x)
    wqkv.own_core()
    for k in range(1, 8):
        net.recv(st_ids[k - 1], st.at[(c + 8 - k) % 8], core)
    means = [st[k, 0:1, :] for k in range(8)]
    mean = sum(means) * 0.125
    total_sq = sum(st[k, 1:2, :] for k in range(8))
    total_sq = total_sq + 768.0 * sum((m - mean) * (m - mean) for m in means)
    inv = lax.rsqrt(total_sq * (1.0 / 6144.0) + EPS)
    sub = lax.broadcasted_iota(jnp.int32, (128, 512), 0)
    columns = jnp.where(sub == 0, mean, jnp.where(sub == 1, inv, 0.0)).T
    lanes = pl.ds(pl.multiple_of(c * 768, 768), 768)
    normed = (tok[...].astype(F32) - columns[:, 0:1]) * columns[:, 1:2]
    modulated = (normed * (1.0 + scale[0:1, lanes]) + shift[0:1, lanes]).astype(BF16)
    mod[...] = modulated
    swap_ids = net.ids(2)
    halves = (pl.ds(0, 256), pl.ds(256, 256))

    xi = net.ids(14)

    def xat(hh, zz, p):
        return Xg.at[4 * hh + zz, halves[p]]

    def xgo(i, ref, device, p, src=None):
        net.send(xi[i], ref if src is None else src, ref, device, lambda: mod.at[halves[p]])

    def xgot(i, ref):
        net.recv(xi[i], ref, core)

    def x_own(src):
        for i, p, device in ((2, 0, zp), (5, 1, zm), (0, 0, xh), (3, 1, zp), (4, 0, zm), (1, 1, xh)):
            xgo(i, xat(h, z, p), device, p, src(p))

    def x_forward():
        xgot(2, xat(h, zb, 0))
        xgo(6, xat(h, zb, 0), zp, 0)
        xgot(5, xat(h, zn, 1))
        xgo(7, xat(h, zn, 1), zm, 1)

    def x_pair(p):
        i, a, b = ((0, 8, 10), (1, 9, 11))[p]
        xgot(i, xat(h2, z, p))
        xgo(a, xat(h2, z, p), zp, p)
        xgo(b, xat(h2, z, p), zm, p)

    def x_forward_pair():
        xgot(8, xat(h2, zb, 0))
        xgo(12, xat(h2, zb, 0), zp, 0)
        xgot(11, xat(h2, zn, 1))
        xgo(13, xat(h2, zn, 1), zm, 1)

    slot = jnp.where(d == l, 0, 1)
    lane_row = lax.broadcasted_iota(jnp.int32, (1, 128), 1).astype(F32)

    def fill(b, carry):
        code = segb[slot, pl.ds(b, 1), :]
        other = jnp.where(lane_row == code, 0.0, 1.0).astype(BF16)
        tile = jnp.broadcast_to(other, (128, 128))
        ones = jnp.ones((128, 128), BF16)
        rows = pl.ds(pl.multiple_of((b % 4) * 128, 128), 128)
        for j in range(3):
            kvx[j, b // 4, rows, 384:512] = tile
            kvx[j, b // 4, rows, 0:128] = ones
        return carry

    def fill_q(b, carry):
        code = segb[slot, pl.ds(4 * rr + b, 1), :]
        same = jnp.where(lane_row == code, -FAR, 0.0).astype(BF16)
        tile = jnp.broadcast_to(same, (128, 128))
        rows = pl.ds(pl.multiple_of(b * 128, 128), 128)
        for j in range(3):
            qx[j, rows, 128:256] = tile
        return carry

    def start_kept():
        x_own(lambda p: mod.at[halves[p]])
        Xg[c] = mod[...]

    def start_traded():
        for p in range(2):
            net.send(swap_ids[p], mod.at[halves[p]], Xg.at[c, halves[p]], sw, lambda p=p: mod.at[halves[p]], True)
        wqkv.own_x()

    both_sides(start_kept, start_traded)
    net.recv(seg_id, segb.at[1], core)
    lax.fori_loop(0, 32, fill, 0)
    lax.fori_loop(0, 4, fill_q, 0)
    wqkv.forward()

    def kept():
        x_forward()
        wqkv.to_core()
        x_pair(0)
        wqkv.far()
        x_pair(1)
        wqkv.pair()
        x_forward_pair()
        wqkv.forward_pair()
        wqkv.pair_to_core()

    def traded():
        wqkv.pair()
        for p in range(2):
            net.recv(swap_ids[p], Xg.at[c, halves[p]], sw)
        x_own(lambda p: None)
        wqkv.to_core()
        x_forward()
        wqkv.far()
        wqkv.forward_pair()
        wqkv.pair_to_core()
        x_pair(0)
        x_pair(1)
        x_forward_pair()

    both_sides(kept, traded)
    wout.own_y()
    wout.own_x()
    wout.own_core()

    a0 = yf
    delta = (zf + 4 - yf) % 4
    third = jnp.where(delta == 0, 1, delta)
    e0 = (a0 + jnp.where(third == 1, 2, 1)) % 4
    e1 = (a0 + jnp.where(third == 3, 2, 3)) % 4
    e2 = (a0 + third) % 4

    def product(block, j):
        left = Xg[block]
        cols = slice(384 * j, 384 * (j + 1))
        right = jnp.concatenate([G[2 * block, :, cols], G[2 * block + 1, :, cols]], axis=0)
        return jnp.dot(left, right, preferred_element_type=F32)

    acc[...] = jnp.zeros_like(acc)
    wqkv.near()
    for i, hh, zz, p in ((3, h, zb, 1), (4, h, zn, 0), (9, h2, zb, 1), (10, h2, zn, 0)):
        xgot(i, xat(hh, zz, p))

    def early(s, carry):
        block = 4 * (s % 2) + jnp.where(s < 2, e0, e1)
        acc[0] += product(block, 0)
        return carry

    lax.fori_loop(0, 4, early, 0)
    wqkv.far_pair()
    xgot(6, xat(h, zf, 0))
    xgot(7, xat(h, zf, 1))
    xgot(12, xat(h2, zf, 0))
    xgot(13, xat(h2, zf, 1))
    wqkv.rest()

    power = (1.0 / HD**0.5) * math.log2(math.e)

    def rms(v):
        return v * lax.rsqrt(jnp.mean(v * v, axis=-1, keepdims=True) + EPS)

    def finish(j):
        def late(s, carry):
            block = 4 * (s % 2) + jnp.where(s < 2, e2, a0)
            acc[j] += product(block, j)
            return carry

        def whole(block, carry):
            acc[j] += product(block, j)
            return carry

        if j == 0:
            lax.fori_loop(0, 4, late, 0)
        else:
            lax.fori_loop(0, 8, whole, 0)
        kvx[j, rr, :, 256:384] = rms(acc[j, :, 128:256]).astype(BF16)
        kvx[j, rr, :, 128:256] = acc[j, :, 256:384].astype(BF16)

    def finish_query(j):
        qx[j, :, 0:128] = (rms(acc[j, :, 0:128]) * (gain[j] * power)).astype(BF16)

    ki = [net.ids(8) for _ in range(3)]

    def kat(j, yy, dd, p=None):
        rows = pl.ds(0, 512) if p is None else halves[p]
        return kvx.at[j, 2 * yy + dd, rows, pl.ds(128, 256)]

    def kgo(j, i, ref, device, p=None):
        like = lambda: kvx.at[0, 0, pl.ds(0, 512) if p is None else halves[p], pl.ds(128, 256)]
        net.send(ki[j][i], ref, ref, device, like)

    def kgot(j, i, ref):
        net.recv(ki[j][i], ref, core)

    def kv_own(j):
        me = kat(j, y, d)
        kgo(j, 0, me, yp)
        kgo(j, 1, me, ym)
        kgo(j, 2, me, core)

    def kv_forward(j):
        kgot(j, 0, kat(j, yb, d))
        kgo(j, 3, kat(j, yb, d, 0), yp, 0)
        kgo(j, 4, kat(j, yb, d), core)
        kgot(j, 1, kat(j, yn, d))
        kgo(j, 5, kat(j, yn, d, 1), ym, 1)
        kgo(j, 6, kat(j, yn, d), core)

    def attend(j, amount, row_of):
        def step(s, carry):
            key_row = row_of(s)
            rows = pl.ds(0, 512)

            @pl.when(jnp.abs(key_row - rr) <= 4)
            def _():
                scores = lax.dot_general(
                    qx[j, rows, :],
                    kvx[j, key_row, :, 256:512],
                    (((1,), (1,)), ((), ())),
                    preferred_element_type=F32,
                )
                weights = jnp.exp2(scores).astype(BF16)
                oacc[rows, :] += jnp.dot(
                    weights, kvx[j, key_row, :, 0:256], preferred_element_type=F32
                )

            return carry

        lax.fori_loop(0, amount, step, 0)

    def kv_far(j):
        kgot(j, 3, kat(j, yf, d, 0))
        kgot(j, 5, kat(j, yf, d, 1))
        kgo(j, 7, kat(j, yf, d), core)
        attend(j, 1, lambda k: 2 * yf + d)

    def attend_here(j):
        oacc[...] = jnp.zeros_like(oacc)
        kgot(j, 2, kat(j, y, 1 - d))
        attend(j, 2, lambda k: 2 * y + k)

    def attend_near(j):
        kgot(j, 4, kat(j, yb, 1 - d))
        kgot(j, 6, kat(j, yn, 1 - d))
        attend(j, 4, lambda k: 2 * ((y + 3 + 2 * (k // 2)) % 4) + k % 2)

    def attend_far(j):
        kgot(j, 7, kat(j, yf, 1 - d))
        attend(j, 1, lambda k: 2 * yf + 1 - d)

    ai = [net.ids(10) for _ in range(3)]

    def aat(j, hh, zz, p=None):
        ref = attg.at[j, 4 * hh + zz]
        return ref if p is None else ref.at[halves[p]]

    def ago(j, i, ref, device, p=None):
        like = lambda: ast.at[0] if p is None else ast.at[0, halves[p]]
        net.send(ai[j][i], ref, ref, device, like)

    def agot(j, i, ref):
        net.recv(ai[j][i], ref, core)

    def att_put(j):
        value = (oacc[:, 128:256] / oacc[:, 0:128]).astype(BF16)

        def keep():
            attg[j, c] = value

        def swap():
            ast[j] = value
            net.send(ai[j][9], ast.at[j], attg.at[j, c], sw, lambda: ast.at[0], True)

        both_sides(keep, swap)

    def att_own(j):
        pl.when(d != l)(lambda: net.recv(ai[j][9], attg.at[j, c], sw))
        me = aat(j, h, z)
        ago(j, 0, me, xh)
        ago(j, 1, me, zp)
        ago(j, 2, me, zm)

    def att_forward(j):
        agot(j, 1, aat(j, h, zb))
        ago(j, 3, aat(j, h, zb, 0), zp, 0)
        agot(j, 2, aat(j, h, zn))
        ago(j, 4, aat(j, h, zn, 1), zm, 1)
        agot(j, 0, aat(j, h2, z))
        ago(j, 5, aat(j, h2, z), zp)
        ago(j, 6, aat(j, h2, z), zm)

    def att_second(j):
        agot(j, 5, aat(j, h2, zb))
        ago(j, 7, aat(j, h2, zb, 0), zp, 0)
        agot(j, 6, aat(j, h2, zn))
        ago(j, 8, aat(j, h2, zn, 1), zm, 1)

    def att_rest(j):
        agot(j, 3, aat(j, h, zf, 0))
        agot(j, 4, aat(j, h, zf, 1))
        agot(j, 7, aat(j, h2, zf, 0))
        agot(j, 8, aat(j, h2, zf, 1))

    def wrows(block, j):
        pieces = []
        for e in range(2):
            unit = 6 * block + 2 * j + e
            pieces.append(woG[unit // 3, pl.ds(pl.multiple_of((unit % 3) * 64, 64), 64), :])
        return pieces

    def project_out(j):
        def step(p, carry):
            left = jnp.concatenate([attg[j, 2 * p], attg[j, 2 * p + 1]], axis=1)
            right = jnp.concatenate(wrows(2 * p, j) + wrows(2 * p + 1, j), axis=0)
            bacc[...] += jnp.dot(left, right, preferred_element_type=F32)
            return carry

        lax.fori_loop(0, 4, step, 0)

    finish(0)
    kv_own(0)
    finish(1)
    kv_own(1)
    finish(2)
    for j in range(3):
        finish_query(j)
    attend_here(0)
    kv_forward(0)
    kv_own(2)
    attend_near(0)
    kv_far(0)
    kv_forward(1)
    attend_far(0)
    att_put(0)
    attend_here(1)
    att_own(0)
    attend_near(1)
    kv_forward(2)
    wout.pair()
    wout.forward()
    kv_far(1)
    att_forward(0)
    attend_far(1)
    att_put(1)
    attend_here(2)
    att_own(1)
    attend_near(2)
    kv_far(2)
    att_second(0)
    attend_far(2)
    att_put(2)
    att_forward(1)
    wout.to_core()
    wout.far()
    att_own(2)
    wout.forward_pair()
    wout.pair_to_core()
    bacc[...] = jnp.zeros_like(bacc)
    att_second(1)
    att_rest(0)
    att_forward(2)
    wout.far_pair()
    att_second(2)
    wout.near()
    wout.rest()
    project_out(0)
    att_rest(1)
    project_out(1)
    att_rest(2)
    project_out(2)
    out[...] = (gate[...] * bacc[...]).astype(BF16)

    for i, (like, some) in net.sent.items():
        if not some:
            net.copy(i, like(), like(), core).wait_send()

    @pl.when(d != l)
    def _():
        for i, (like, some) in net.sent.items():
            if some:
                net.copy(i, like(), like(), core).wait_send()


def local(tokens, w_qkv, w_out, ada_shift, ada_scale, out_gate, head_gain, block_segment):
    vmem = pl.BlockSpec(memory_space=pltpu.VMEM)
    smem = pl.BlockSpec(memory_space=pltpu.SMEM)
    anyw = pl.BlockSpec(memory_space=pl.ANY)
    return pl.pallas_call(
        kernel,
        out_shape=jax.ShapeDtypeStruct((512, 768), BF16),
        in_specs=[anyw] * 3 + [vmem] * 3 + [smem] * 2,
        out_specs=vmem,
        scratch_shapes=[
            pltpu.VMEM((512, 768), BF16),
            pltpu.VMEM((16, 384, 1152), BF16),
            pltpu.VMEM((8, 512, 768), BF16),
            pltpu.VMEM((3, 8, 512, 512), BF16),
            pltpu.VMEM((3, 512, 256), BF16),
            pltpu.VMEM((16, 192, 768), BF16),
            pltpu.VMEM((3, 8, 512, 128), BF16),
            pltpu.VMEM((3, 512, 384), F32),
            pltpu.VMEM((512, 256), F32),
            pltpu.VMEM((512, 768), F32),
            pltpu.VMEM((512, 768), BF16),
            pltpu.VMEM((3, 512, 128), BF16),
            pltpu.VMEM((8, 8, 512), F32),
            pltpu.VMEM((2, 32, 128), F32),
            pltpu.SemaphoreType.DMA((N_FLOWS,)),
            pltpu.SemaphoreType.DMA((N_FLOWS,)),
            pltpu.SemaphoreType.DMA((3,)),
        ],
        compiler_params=pltpu.CompilerParams(
            collective_id=0, has_side_effects=True, vmem_limit_bytes=60 * 2**20
        ),
    )(tokens, w_qkv, w_out, ada_shift, ada_scale, out_gate, head_gain, block_segment)


def solution(mesh):
    placed = (
        P(("dp", "row"), "col"),
        P(("dp", "row"), "col"),
        P(("dp", "row"), "col"),
        P("dp", None),
        P("dp", None),
        P("dp", "col"),
        P("col"),
        P("dp", None),
    )
    return jax.shard_map(
        local, mesh=mesh, in_specs=placed, out_specs=P(("dp", "row"), "col"), check_vma=False
    )
```

```python
import math

import jax
import jax.numpy as jnp
from jax import lax
from jax.experimental import pallas as pl
from jax.experimental.pallas import tpu as pltpu
from jax.sharding import PartitionSpec as P

HD = 128
BLK = 128
EPS = 1e-06
FAR = 2048.0
F32 = jnp.float32
BF16 = jnp.bfloat16
MESH = pl.DeviceIdType.MESH
N_FLOWS = 160


class Net:
    def __init__(self, ss, rs):
        self.ss, self.rs, self.count, self.sent = ss, rs, 0, {}

    def ids(self, amount):
        first = self.count
        self.count += amount
        assert self.count <= N_FLOWS
        return list(range(first, self.count))

    def copy(self, i, src, dst, device):
        return pltpu.make_async_remote_copy(
            src_ref=src,
            dst_ref=dst,
            send_sem=self.ss.at[i],
            recv_sem=self.rs.at[i],
            device_id=device,
            device_id_type=MESH,
        )

    def send(self, i, src, dst, device, like, some=False):
        self.copy(i, src, dst, device).start()
        self.sent[i] = (like, some)

    def recv(self, i, ref, device):
        self.copy(i, ref, ref, device).wait_recv()


def kernel(
    tok_hbm, wq, wo, shift, scale, gate, gain, seg, out,
    tok, G, Xg, kvx, qx, woG, attg, acc, oacc, bacc, mod, ast, st, segb, ss, rs, ls,
):
    d, row, c = lax.axis_index("dp"), lax.axis_index("row"), lax.axis_index("col")
    y, l = row // 2, row % 2
    h, z = c // 4, c % 4
    yn, yf, yb = (y + 1) % 4, (y + 2) % 4, (y + 3) % 4
    zn, zf, zb = (z + 1) % 4, (z + 2) % 4, (z + 3) % 4
    h2 = 1 - h
    core = (1 - d, row, c)
    xl = (d, 2 * y + 1 - l, c)
    yp, ym = (d, 2 * yn + l, c), (d, 2 * yb + l, c)
    zp, zm = (d, row, 4 * h + zn), (d, row, 4 * h + zb)
    xh = (d, row, 4 * h2 + z)
    sw = (l, 2 * y + d, c)
    rr = 2 * y + d
    net = Net(ss, rs)

    def both_sides(first, second):
        pl.when(d == l)(first)
        pl.when(d != l)(second)

    tok_copy = pltpu.make_async_copy(tok_hbm, tok, ls.at[2])
    tok_copy.start()

    barrier = pltpu.get_barrier_semaphore()
    z_peers = [(d, row, 4 * h + (z + k) % 4) for k in range(1, 4)]
    for peer in z_peers + [xh, core, xl, yp, ym]:
        pl.semaphore_signal(barrier, inc=1, device_id=peer, device_id_type=MESH)

    @pl.when(d != l)
    def _():
        pl.semaphore_signal(barrier, inc=1, device_id=sw, device_id_type=MESH)

    for b in range(32):
        segb[0, b : b + 1, :] = jnp.full((1, 128), seg[0, b], jnp.int32).astype(F32)

    tok_copy.wait()
    x = tok[...].astype(F32)
    part_mean = jnp.sum(x, axis=-1, keepdims=True) * (1.0 / 768.0)
    off = x - part_mean
    part_sq = jnp.sum(off * off, axis=-1, keepdims=True)
    lane = lax.broadcasted_iota(jnp.int32, (512, 128), 1)
    columns = jnp.where(lane == 0, part_mean, jnp.where(lane == 1, part_sq, 0.0))
    st[z, h] = columns.T[:8]
    pl.semaphore_wait(barrier, 8 + (d + l) % 2)

    def wid(dd, yy, ll):
        return 8 * dd + 2 * yy + ll

    class Weight:
        def __init__(self, src, dst, rows, local_sem):
            self.src, self.dst, self.half = src, dst, rows // 2
            self.parts = {None: pl.ds(0, rows), 0: pl.ds(0, rows // 2), 1: pl.ds(rows // 2, rows // 2)}
            self.f = dict(zip(self.names, net.ids(len(self.names))))
            self.local = pltpu.make_async_copy(src, dst.at[wid(d, y, l)], local_sem)

        names = (
            "own_yp0", "own_yp1", "own_ym0", "own_ym1", "own_xl0", "own_xl1",
            "own_core", "fwd_yp", "fwd_ym", "core_yb", "core_yn", "pair_yp0",
            "pair_yp1", "pair_ym0", "pair_ym1", "core_pair", "last_yp", "last_ym",
            "core_yb2", "core_yn2", "far0", "far1", "far2", "far3",
        )

        def at(self, dd, yy, ll, part=None):
            return self.dst.at[wid(dd, yy, ll), self.parts[part]]

        def go(self, name, device, dd, yy, ll, part=None, src=None):
            ref = self.at(dd, yy, ll, part)
            like = lambda: self.dst.at[0, self.parts[part]]
            net.send(self.f[name], ref if src is None else src, ref, device, like)

        def got(self, name, dd, yy, ll, part=None):
            net.recv(self.f[name], self.at(dd, yy, ll, part), core)

        def own(self, name, device, part=None):
            self.go(name, device, d, y, l, part, self.src.at[self.parts[part]])

        def own_y(self):
            self.own("own_yp0", yp, 0)
            self.own("own_ym1", ym, 1)
            self.own("own_yp1", yp, 1)
            self.own("own_ym0", ym, 0)

        def own_core(self):
            self.own("own_core", core)
            self.local.start()

        def own_x(self):
            self.own("own_xl0", xl, 0)
            self.own("own_xl1", xl, 1)

        def forward(self):
            self.got("own_yp0", d, yb, l, 0)
            self.go("fwd_yp", yp, d, yb, l, 0)
            self.got("own_ym1", d, yn, l, 1)
            self.go("fwd_ym", ym, d, yn, l, 1)

        def to_core(self):
            self.got("own_yp1", d, yb, l, 1)
            self.go("core_yb", core, d, yb, l)
            self.got("own_ym0", d, yn, l, 0)
            self.go("core_yn", core, d, yn, l)

        def pair(self):
            for p in range(2):
                self.got(f"own_xl{p}", d, y, 1 - l, p)
                self.go(f"pair_yp{p}", yp, d, y, 1 - l, p)
                self.go(f"pair_ym{p}", ym, d, y, 1 - l, p)
            self.go("core_pair", core, d, y, 1 - l)

        def forward_pair(self):
            self.got("pair_yp0", d, yb, 1 - l, 0)
            self.go("last_yp", yp, d, yb, 1 - l, 0)
            self.got("pair_ym1", d, yn, 1 - l, 1)
            self.go("last_ym", ym, d, yn, 1 - l, 1)

        def pair_to_core(self):
            self.got("pair_yp1", d, yb, 1 - l, 1)
            self.go("core_yb2", core, d, yb, 1 - l)
            self.got("pair_ym0", d, yn, 1 - l, 0)
            self.go("core_yn2", core, d, yn, 1 - l)

        def far(self):
            self.got("fwd_yp", d, yf, l, 0)
            self.go("far0", core, d, yf, l, 0)
            self.got("fwd_ym", d, yf, l, 1)
            self.go("far1", core, d, yf, l, 1)

        def far_pair(self):
            self.got("last_yp", d, yf, 1 - l, 0)
            self.go("far2", core, d, yf, 1 - l, 0)
            self.got("last_ym", d, yf, 1 - l, 1)
            self.go("far3", core, d, yf, 1 - l, 1)

        def near(self):
            self.local.wait()
            self.got("own_core", 1 - d, y, l)
            self.got("core_yb", 1 - d, yb, l)
            self.got("core_yn", 1 - d, yn, l)
            self.got("core_pair", 1 - d, y, 1 - l)
            self.got("core_yb2", 1 - d, yb, 1 - l)
            self.got("core_yn2", 1 - d, yn, 1 - l)

        def rest(self):
            for p in range(2):
                self.got(f"far{p}", 1 - d, yf, l, p)
                self.got(f"far{2 + p}", 1 - d, yf, 1 - l, p)

    wqkv = Weight(wq, G, 384, ls.at[0])
    wout = Weight(wo, woG, 192, ls.at[1])

    st_ids = net.ids(4)
    net.send(st_ids[0], st.at[z, h], st.at[z, h], xh, lambda: st.at[0, 0])
    seg_id = net.ids(1)[0]
    net.send(seg_id, segb.at[0], segb.at[1], core, lambda: segb.at[0])
    wqkv.own_y()
    pl.when(d == l)(wqkv.own_x)
    wqkv.own_core()
    net.recv(st_ids[0], st.at[z, h2], xh)
    for k in range(1, 4):
        net.send(st_ids[k], st.at[z], st.at[z], z_peers[k - 1], lambda: st.at[0])
    for k in range(1, 4):
        net.recv(st_ids[k], st.at[(z + 4 - k) % 4], core)
    means = [st[k // 2, k % 2, 0:1, :] for k in range(8)]
    mean = sum(means) * 0.125
    total_sq = sum(st[k // 2, k % 2, 1:2, :] for k in range(8))
    total_sq = total_sq + 768.0 * sum((m - mean) * (m - mean) for m in means)
    inv = lax.rsqrt(total_sq * (1.0 / 6144.0) + EPS)
    sub = lax.broadcasted_iota(jnp.int32, (128, 512), 0)
    columns = jnp.where(sub == 0, mean, jnp.where(sub == 1, inv, 0.0)).T
    lanes = pl.ds(pl.multiple_of(c * 768, 768), 768)
    normed = (tok[...].astype(F32) - columns[:, 0:1]) * columns[:, 1:2]
    modulated = (normed * (1.0 + scale[0:1, lanes]) + shift[0:1, lanes]).astype(BF16)
    mod[...] = modulated
    swap_ids = net.ids(2)
    halves = (pl.ds(0, 256), pl.ds(256, 256))

    xi = net.ids(14)

    def xat(hh, zz, p):
        return Xg.at[4 * hh + zz, halves[p]]

    def xgo(i, ref, device, p, src=None):
        net.send(xi[i], ref if src is None else src, ref, device, lambda: mod.at[halves[p]])

    def xgot(i, ref):
        net.recv(xi[i], ref, core)

    def x_own(src):
        for i, p, device in ((2, 0, zp), (5, 1, zm), (0, 0, xh), (3, 1, zp), (4, 0, zm), (1, 1, xh)):
            xgo(i, xat(h, z, p), device, p, src(p))

    def x_forward():
        xgot(2, xat(h, zb, 0))
        xgo(6, xat(h, zb, 0), zp, 0)
        xgot(5, xat(h, zn, 1))
        xgo(7, xat(h, zn, 1), zm, 1)

    def x_pair(p):
        i, a, b = ((0, 8, 10), (1, 9, 11))[p]
        xgot(i, xat(h2, z, p))
        xgo(a, xat(h2, z, p), zp, p)
        xgo(b, xat(h2, z, p), zm, p)

    def x_forward_pair():
        xgot(8, xat(h2, zb, 0))
        xgo(12, xat(h2, zb, 0), zp, 0)
        xgot(11, xat(h2, zn, 1))
        xgo(13, xat(h2, zn, 1), zm, 1)

    slot = jnp.where(d == l, 0, 1)
    lane_row = lax.broadcasted_iota(jnp.int32, (1, 128), 1).astype(F32)

    def fill(b, carry):
        code = segb[slot, pl.ds(b, 1), :]
        other = jnp.where(lane_row == code, 0.0, 1.0).astype(BF16)
        tile = jnp.broadcast_to(other, (128, 128))
        ones = jnp.ones((128, 128), BF16)
        rows = pl.ds(pl.multiple_of((b % 4) * 128, 128), 128)
        for j in range(3):
            kvx[j, b // 4, rows, 384:512] = tile
            kvx[j, b // 4, rows, 0:128] = ones
        return carry

    def fill_q(b, carry):
        code = segb[slot, pl.ds(4 * rr + b, 1), :]
        same = jnp.where(lane_row == code, -FAR, 0.0).astype(BF16)
        tile = jnp.broadcast_to(same, (128, 128))
        rows = pl.ds(pl.multiple_of(b * 128, 128), 128)
        for j in range(3):
            qx[j, rows, 128:256] = tile
        return carry

    def start_kept():
        x_own(lambda p: mod.at[halves[p]])
        Xg[c] = mod[...]

    def start_traded():
        for p in range(2):
            net.send(swap_ids[p], mod.at[halves[p]], Xg.at[c, halves[p]], sw, lambda p=p: mod.at[halves[p]], True)
        wqkv.own_x()

    both_sides(start_kept, start_traded)
    net.recv(seg_id, segb.at[1], core)
    lax.fori_loop(0, 32, fill, 0)
    lax.fori_loop(0, 4, fill_q, 0)
    wqkv.forward()

    def kept():
        x_forward()
        wqkv.to_core()
        x_pair(0)
        wqkv.far()
        x_pair(1)
        wqkv.pair()
        x_forward_pair()
        wqkv.forward_pair()
        wqkv.pair_to_core()

    def traded():
        wqkv.pair()
        for p in range(2):
            net.recv(swap_ids[p], Xg.at[c, halves[p]], sw)
        x_own(lambda p: None)
        wqkv.to_core()
        x_forward()
        wqkv.far()
        wqkv.forward_pair()
        wqkv.pair_to_core()
        x_pair(0)
        x_pair(1)
        x_forward_pair()

    both_sides(kept, traded)
    wout.own_y()
    wout.own_x()
    wout.own_core()

    a0 = yf
    delta = (zf + 4 - yf) % 4
    third = jnp.where(delta == 0, 1, delta)
    e0 = (a0 + jnp.where(third == 1, 2, 1)) % 4
    e1 = (a0 + jnp.where(third == 3, 2, 3)) % 4
    e2 = (a0 + third) % 4

    def product(block, j):
        left = Xg[block]
        cols = slice(384 * j, 384 * (j + 1))
        right = jnp.concatenate([G[2 * block, :, cols], G[2 * block + 1, :, cols]], axis=0)
        return jnp.dot(left, right, preferred_element_type=F32)

    acc[...] = jnp.zeros_like(acc)
    wqkv.near()
    for i, hh, zz, p in ((3, h, zb, 1), (4, h, zn, 0), (9, h2, zb, 1), (10, h2, zn, 0)):
        xgot(i, xat(hh, zz, p))

    def early(s, carry):
        block = 4 * (s % 2) + jnp.where(s < 2, e0, e1)
        acc[0] += product(block, 0)
        return carry

    lax.fori_loop(0, 4, early, 0)
    wqkv.far_pair()
    xgot(6, xat(h, zf, 0))
    xgot(7, xat(h, zf, 1))
    xgot(12, xat(h2, zf, 0))
    xgot(13, xat(h2, zf, 1))
    wqkv.rest()

    power = (1.0 / HD**0.5) * math.log2(math.e)

    def rms(v):
        return v * lax.rsqrt(jnp.mean(v * v, axis=-1, keepdims=True) + EPS)

    def finish(j):
        def late(s, carry):
            block = 4 * (s % 2) + jnp.where(s < 2, e2, a0)
            acc[j] += product(block, j)
            return carry

        def whole(block, carry):
            acc[j] += product(block, j)
            return carry

        if j == 0:
            lax.fori_loop(0, 4, late, 0)
        else:
            lax.fori_loop(0, 8, whole, 0)
        kvx[j, rr, :, 256:384] = rms(acc[j, :, 128:256]).astype(BF16)
        kvx[j, rr, :, 128:256] = acc[j, :, 256:384].astype(BF16)

    def finish_query(j):
        qx[j, :, 0:128] = (rms(acc[j, :, 0:128]) * gain[j]).astype(BF16)

    ki = [net.ids(8) for _ in range(3)]

    def kat(j, yy, dd, p=None):
        rows = pl.ds(0, 512) if p is None else halves[p]
        return kvx.at[j, 2 * yy + dd, rows, pl.ds(128, 256)]

    def kgo(j, i, ref, device, p=None):
        like = lambda: kvx.at[0, 0, pl.ds(0, 512) if p is None else halves[p], pl.ds(128, 256)]
        net.send(ki[j][i], ref, ref, device, like)

    def kgot(j, i, ref):
        net.recv(ki[j][i], ref, core)

    def kv_own(j):
        me = kat(j, y, d)
        kgo(j, 0, me, yp)
        kgo(j, 1, me, ym)
        kgo(j, 2, me, core)

    def kv_forward(j):
        kgot(j, 0, kat(j, yb, d))
        kgo(j, 3, kat(j, yb, d, 0), yp, 0)
        kgo(j, 4, kat(j, yb, d), core)
        kgot(j, 1, kat(j, yn, d))
        kgo(j, 5, kat(j, yn, d, 1), ym, 1)
        kgo(j, 6, kat(j, yn, d), core)

    def attend(j, amount, row_of):
        def step(s, carry):
            key_row = row_of(s)
            rows = pl.ds(0, 512)

            @pl.when(jnp.abs(key_row - rr) <= 4)
            def _():
                scores = lax.dot_general(
                    qx[j, rows, :],
                    kvx[j, key_row, :, 256:512],
                    (((1,), (1,)), ((), ())),
                    preferred_element_type=F32,
                )
                weights = jnp.exp2(scores * power).astype(BF16)
                oacc[rows, :] += jnp.dot(
                    weights, kvx[j, key_row, :, 0:256], preferred_element_type=F32
                )

            return carry

        lax.fori_loop(0, amount, step, 0)

    def kv_far(j):
        kgot(j, 3, kat(j, yf, d, 0))
        kgot(j, 5, kat(j, yf, d, 1))
        kgo(j, 7, kat(j, yf, d), core)
        attend(j, 1, lambda k: 2 * yf + d)

    def attend_here(j):
        oacc[...] = jnp.zeros_like(oacc)
        kgot(j, 2, kat(j, y, 1 - d))
        attend(j, 2, lambda k: 2 * y + k)

    def attend_near(j):
        kgot(j, 4, kat(j, yb, 1 - d))
        kgot(j, 6, kat(j, yn, 1 - d))
        attend(j, 4, lambda k: 2 * ((y + 3 + 2 * (k // 2)) % 4) + k % 2)

    def attend_far(j):
        kgot(j, 7, kat(j, yf, 1 - d))
        attend(j, 1, lambda k: 2 * yf + 1 - d)

    ai = [net.ids(16) for _ in range(3)]

    def aat(j, hh, zz, p):
        return attg.at[j, 4 * hh + zz, halves[p]]

    def ago(j, i, hh, zz, p, device):
        net.send(ai[j][i], aat(j, hh, zz, p), aat(j, hh, zz, p), device, lambda: ast.at[0, halves[p]])

    def agot(j, i, hh, zz, p):
        net.recv(ai[j][i], aat(j, hh, zz, p), core)

    def att_send(j, p):
        for i, device in (((2, zp), (0, xh), (4, zm)), ((5, zm), (1, xh), (3, zp)))[p]:
            ago(j, i, h, z, p, device)

    def att_put(j):
        def keep(p, value):
            attg[j, c, halves[p], :] = value
            att_send(j, p)

        def swap(p, value):
            ast[j, halves[p], :] = value
            like = lambda: ast.at[0, halves[p]]
            net.send(ai[j][14 + p], ast.at[j, halves[p]], attg.at[j, c, halves[p]], sw, like, True)

        for p in range(2):
            value = (oacc[halves[p], 128:256] / oacc[halves[p], 0:128]).astype(BF16)
            pl.when(d == l)(lambda: keep(p, value))
            pl.when(d != l)(lambda: swap(p, value))

    def att_own(j):
        def traded_own():
            for p in range(2):
                agot(j, 14 + p, h, z, p)
                att_send(j, p)

        pl.when(d != l)(traded_own)

    def att_forward(j):
        agot(j, 2, h, zb, 0)
        ago(j, 6, h, zb, 0, zp)
        agot(j, 5, h, zn, 1)
        ago(j, 7, h, zn, 1, zm)
        agot(j, 0, h2, z, 0)
        ago(j, 8, h2, z, 0, zp)
        ago(j, 10, h2, z, 0, zm)
        agot(j, 1, h2, z, 1)
        ago(j, 11, h2, z, 1, zm)
        ago(j, 9, h2, z, 1, zp)

    def att_second(j):
        agot(j, 8, h2, zb, 0)
        ago(j, 12, h2, zb, 0, zp)
        agot(j, 11, h2, zn, 1)
        ago(j, 13, h2, zn, 1, zm)

    def att_rest(j):
        agot(j, 3, h, zb, 1)
        agot(j, 4, h, zn, 0)
        agot(j, 9, h2, zb, 1)
        agot(j, 10, h2, zn, 0)
        for p in range(2):
            agot(j, 6 + p, h, zf, p)
            agot(j, 12 + p, h2, zf, p)

    def wrows(block, j):
        pieces = []
        for e in range(2):
            unit = 6 * block + 2 * j + e
            pieces.append(woG[unit // 3, pl.ds(pl.multiple_of((unit % 3) * 64, 64), 64), :])
        return pieces

    def project_out(j):
        def step(p, carry):
            left = jnp.concatenate([attg[j, 2 * p], attg[j, 2 * p + 1]], axis=1)
            right = jnp.concatenate(wrows(2 * p, j) + wrows(2 * p + 1, j), axis=0)
            bacc[...] += jnp.dot(left, right, preferred_element_type=F32)
            return carry

        lax.fori_loop(0, 4, step, 0)

    finish(0)
    kv_own(0)
    finish(1)
    kv_own(1)
    finish(2)
    for j in range(3):
        finish_query(j)
    attend_here(0)
    kv_forward(0)
    kv_own(2)
    attend_near(0)
    kv_far(0)
    kv_forward(1)
    attend_far(0)
    att_put(0)
    attend_here(1)
    att_own(0)
    attend_near(1)
    kv_forward(2)
    wout.pair()
    wout.forward()
    kv_far(1)
    att_forward(0)
    attend_far(1)
    att_put(1)
    attend_here(2)
    att_own(1)
    attend_near(2)
    kv_far(2)
    att_second(0)
    attend_far(2)
    att_put(2)
    wout.to_core()
    att_forward(1)
    att_own(2)
    wout.far()
    wout.forward_pair()
    wout.pair_to_core()
    bacc[...] = jnp.zeros_like(bacc)
    att_second(1)
    att_rest(0)
    att_forward(2)
    wout.far_pair()
    att_second(2)
    wout.near()
    wout.rest()
    project_out(0)
    att_rest(1)
    project_out(1)
    att_rest(2)
    project_out(2)
    out[...] = (gate[...] * bacc[...]).astype(BF16)

    for i, (like, some) in net.sent.items():
        if not some:
            net.copy(i, like(), like(), core).wait_send()

    @pl.when(d != l)
    def _():
        for i, (like, some) in net.sent.items():
            if some:
                net.copy(i, like(), like(), core).wait_send()


def local(tokens, w_qkv, w_out, ada_shift, ada_scale, out_gate, head_gain, block_segment):
    vmem = pl.BlockSpec(memory_space=pltpu.VMEM)
    smem = pl.BlockSpec(memory_space=pltpu.SMEM)
    anyw = pl.BlockSpec(memory_space=pl.ANY)
    return pl.pallas_call(
        kernel,
        out_shape=jax.ShapeDtypeStruct((512, 768), BF16),
        in_specs=[anyw] * 3 + [vmem] * 3 + [smem] * 2,
        out_specs=vmem,
        scratch_shapes=[
            pltpu.VMEM((512, 768), BF16),
            pltpu.VMEM((16, 384, 1152), BF16),
            pltpu.VMEM((8, 512, 768), BF16),
            pltpu.VMEM((3, 8, 512, 512), BF16),
            pltpu.VMEM((3, 512, 256), BF16),
            pltpu.VMEM((16, 192, 768), BF16),
            pltpu.VMEM((3, 8, 512, 128), BF16),
            pltpu.VMEM((3, 512, 384), F32),
            pltpu.VMEM((512, 256), F32),
            pltpu.VMEM((512, 768), F32),
            pltpu.VMEM((512, 768), BF16),
            pltpu.VMEM((3, 512, 128), BF16),
            pltpu.VMEM((4, 2, 8, 512), F32),
            pltpu.VMEM((2, 32, 128), F32),
            pltpu.SemaphoreType.DMA((N_FLOWS,)),
            pltpu.SemaphoreType.DMA((N_FLOWS,)),
            pltpu.SemaphoreType.DMA((3,)),
        ],
        compiler_params=pltpu.CompilerParams(
            collective_id=0, has_side_effects=True, vmem_limit_bytes=60 * 2**20
        ),
    )(tokens, w_qkv, w_out, ada_shift, ada_scale, out_gate, head_gain, block_segment)


def solution(mesh):
    placed = (
        P(("dp", "row"), "col"),
        P(("dp", "row"), "col"),
        P(("dp", "row"), "col"),
        P("dp", None),
        P("dp", None),
        P("dp", "col"),
        P("col"),
        P("dp", None),
    )
    return jax.shard_map(
        local, mesh=mesh, in_specs=placed, out_specs=P(("dp", "row"), "col"), check_vma=False
    )
```

```python
import math

import jax
import jax.numpy as jnp
from jax import lax
from jax.experimental import pallas as pl
from jax.experimental.pallas import tpu as pltpu
from jax.sharding import PartitionSpec as P

HD = 128
BLK = 128
EPS = 1e-06
FAR = 2048.0
F32 = jnp.float32
BF16 = jnp.bfloat16
MESH = pl.DeviceIdType.MESH
N_FLOWS = 160


class Net:
    def __init__(self, ss, rs):
        self.ss, self.rs, self.count, self.sent = ss, rs, 0, {}

    def ids(self, amount):
        first = self.count
        self.count += amount
        assert self.count <= N_FLOWS
        return list(range(first, self.count))

    def copy(self, i, src, dst, device):
        return pltpu.make_async_remote_copy(
            src_ref=src,
            dst_ref=dst,
            send_sem=self.ss.at[i],
            recv_sem=self.rs.at[i],
            device_id=device,
            device_id_type=MESH,
        )

    def send(self, i, src, dst, device, like, some=False):
        self.copy(i, src, dst, device).start()
        self.sent[i] = (like, some)

    def recv(self, i, ref, device):
        self.copy(i, ref, ref, device).wait_recv()


def kernel(
    tok_hbm, wq, wo, shift, scale, gate, gain, seg, out,
    tok, G, Xg, kvx, qx, woG, attg, acc, oacc, bacc, mod, ast, st, segb, ss, rs, ls,
):
    d, row, c = lax.axis_index("dp"), lax.axis_index("row"), lax.axis_index("col")
    y, l = row // 2, row % 2
    h, z = c // 4, c % 4
    yn, yf, yb = (y + 1) % 4, (y + 2) % 4, (y + 3) % 4
    zn, zf, zb = (z + 1) % 4, (z + 2) % 4, (z + 3) % 4
    h2 = 1 - h
    core = (1 - d, row, c)
    xl = (d, 2 * y + 1 - l, c)
    yp, ym = (d, 2 * yn + l, c), (d, 2 * yb + l, c)
    zp, zm = (d, row, 4 * h + zn), (d, row, 4 * h + zb)
    xh = (d, row, 4 * h2 + z)
    sw = (l, 2 * y + d, c)
    rr = 2 * y + d
    net = Net(ss, rs)

    def both_sides(first, second):
        pl.when(d == l)(first)
        pl.when(d != l)(second)

    tok_copy = pltpu.make_async_copy(tok_hbm, tok, ls.at[2])
    tok_copy.start()

    barrier = pltpu.get_barrier_semaphore()
    z_peers = [(d, row, 4 * h + (z + k) % 4) for k in range(1, 4)]
    for peer in z_peers + [xh, core, xl, yp, ym]:
        pl.semaphore_signal(barrier, inc=1, device_id=peer, device_id_type=MESH)

    @pl.when(d != l)
    def _():
        pl.semaphore_signal(barrier, inc=1, device_id=sw, device_id_type=MESH)

    for b in range(32):
        segb[0, b : b + 1, :] = jnp.full((1, 128), seg[0, b], jnp.int32).astype(F32)

    tok_copy.wait()
    x = tok[...].astype(F32)
    part_mean = jnp.sum(x, axis=-1, keepdims=True) * (1.0 / 768.0)
    off = x - part_mean
    part_sq = jnp.sum(off * off, axis=-1, keepdims=True)
    lane = lax.broadcasted_iota(jnp.int32, (512, 128), 1)
    columns = jnp.where(lane == 0, part_mean, jnp.where(lane == 1, part_sq, 0.0))
    st[z, h] = columns.T[:8]
    pl.semaphore_wait(barrier, 8 + (d + l) % 2)

    def wid(dd, yy, ll):
        return 8 * dd + 2 * yy + ll

    class Weight:
        def __init__(self, src, dst, rows, local_sem):
            self.src, self.dst, self.half = src, dst, rows // 2
            self.parts = {None: pl.ds(0, rows), 0: pl.ds(0, rows // 2), 1: pl.ds(rows // 2, rows // 2)}
            self.f = dict(zip(self.names, net.ids(len(self.names))))
            self.local = pltpu.make_async_copy(src, dst.at[wid(d, y, l)], local_sem)

        names = (
            "own_yp0", "own_yp1", "own_ym0", "own_ym1", "own_xl0", "own_xl1",
            "own_core", "fwd_yp", "fwd_ym", "core_yb", "core_yn", "pair_yp0",
            "pair_yp1", "pair_ym0", "pair_ym1", "core_pair", "last_yp", "last_ym",
            "core_yb2", "core_yn2", "far0", "far1", "far2", "far3",
        )

        def at(self, dd, yy, ll, part=None):
            return self.dst.at[wid(dd, yy, ll), self.parts[part]]

        def go(self, name, device, dd, yy, ll, part=None, src=None):
            ref = self.at(dd, yy, ll, part)
            like = lambda: self.dst.at[0, self.parts[part]]
            net.send(self.f[name], ref if src is None else src, ref, device, like)

        def got(self, name, dd, yy, ll, part=None):
            net.recv(self.f[name], self.at(dd, yy, ll, part), core)

        def own(self, name, device, part=None):
            self.go(name, device, d, y, l, part, self.src.at[self.parts[part]])

        def own_y(self):
            self.own("own_yp0", yp, 0)
            self.own("own_ym1", ym, 1)
            self.own("own_yp1", yp, 1)
            self.own("own_ym0", ym, 0)

        def own_core(self):
            self.own("own_core", core)
            self.local.start()

        def own_x(self):
            self.own("own_xl0", xl, 0)
            self.own("own_xl1", xl, 1)

        def forward(self):
            self.got("own_yp0", d, yb, l, 0)
            self.go("fwd_yp", yp, d, yb, l, 0)
            self.got("own_ym1", d, yn, l, 1)
            self.go("fwd_ym", ym, d, yn, l, 1)

        def to_core(self):
            self.got("own_yp1", d, yb, l, 1)
            self.go("core_yb", core, d, yb, l)
            self.got("own_ym0", d, yn, l, 0)
            self.go("core_yn", core, d, yn, l)

        def pair(self):
            for p in range(2):
                self.got(f"own_xl{p}", d, y, 1 - l, p)
                self.go(f"pair_yp{p}", yp, d, y, 1 - l, p)
                self.go(f"pair_ym{p}", ym, d, y, 1 - l, p)
            self.go("core_pair", core, d, y, 1 - l)

        def forward_pair(self):
            self.got("pair_yp0", d, yb, 1 - l, 0)
            self.go("last_yp", yp, d, yb, 1 - l, 0)
            self.got("pair_ym1", d, yn, 1 - l, 1)
            self.go("last_ym", ym, d, yn, 1 - l, 1)

        def pair_to_core(self):
            self.got("pair_yp1", d, yb, 1 - l, 1)
            self.go("core_yb2", core, d, yb, 1 - l)
            self.got("pair_ym0", d, yn, 1 - l, 0)
            self.go("core_yn2", core, d, yn, 1 - l)

        def far(self):
            self.got("fwd_yp", d, yf, l, 0)
            self.go("far0", core, d, yf, l, 0)
            self.got("fwd_ym", d, yf, l, 1)
            self.go("far1", core, d, yf, l, 1)

        def far_pair(self):
            self.got("last_yp", d, yf, 1 - l, 0)
            self.go("far2", core, d, yf, 1 - l, 0)
            self.got("last_ym", d, yf, 1 - l, 1)
            self.go("far3", core, d, yf, 1 - l, 1)

        def near(self):
            self.local.wait()
            self.got("own_core", 1 - d, y, l)
            self.got("core_yb", 1 - d, yb, l)
            self.got("core_yn", 1 - d, yn, l)
            self.got("core_pair", 1 - d, y, 1 - l)
            self.got("core_yb2", 1 - d, yb, 1 - l)
            self.got("core_yn2", 1 - d, yn, 1 - l)

        def rest(self):
            for p in range(2):
                self.got(f"far{p}", 1 - d, yf, l, p)
                self.got(f"far{2 + p}", 1 - d, yf, 1 - l, p)

    wqkv = Weight(wq, G, 384, ls.at[0])
    wout = Weight(wo, woG, 192, ls.at[1])

    st_ids = net.ids(4)
    net.send(st_ids[0], st.at[z, h], st.at[z, h], xh, lambda: st.at[0, 0])
    seg_id = net.ids(1)[0]
    net.send(seg_id, segb.at[0], segb.at[1], core, lambda: segb.at[0])
    wqkv.own_y()
    pl.when(d == l)(wqkv.own_x)
    wqkv.own_core()
    net.recv(st_ids[0], st.at[z, h2], xh)
    for k in range(1, 4):
        net.send(st_ids[k], st.at[z], st.at[z], z_peers[k - 1], lambda: st.at[0])
    for k in range(1, 4):
        net.recv(st_ids[k], st.at[(z + 4 - k) % 4], core)
    means = [st[k // 2, k % 2, 0:1, :] for k in range(8)]
    mean = sum(means) * 0.125
    total_sq = sum(st[k // 2, k % 2, 1:2, :] for k in range(8))
    total_sq = total_sq + 768.0 * sum((m - mean) * (m - mean) for m in means)
    inv = lax.rsqrt(total_sq * (1.0 / 6144.0) + EPS)
    sub = lax.broadcasted_iota(jnp.int32, (128, 512), 0)
    columns = jnp.where(sub == 0, mean, jnp.where(sub == 1, inv, 0.0)).T
    lanes = pl.ds(pl.multiple_of(c * 768, 768), 768)
    normed = (tok[...].astype(F32) - columns[:, 0:1]) * columns[:, 1:2]
    modulated = (normed * (1.0 + scale[0:1, lanes]) + shift[0:1, lanes]).astype(BF16)
    mod[...] = modulated
    swap_ids = net.ids(2)
    halves = (pl.ds(0, 256), pl.ds(256, 256))

    xi = net.ids(14)

    def xat(hh, zz, p):
        return Xg.at[4 * hh + zz, halves[p]]

    def xgo(i, ref, device, p, src=None):
        net.send(xi[i], ref if src is None else src, ref, device, lambda: mod.at[halves[p]])

    def xgot(i, ref):
        net.recv(xi[i], ref, core)

    def x_own(src):
        for i, p, device in ((2, 0, zp), (5, 1, zm), (0, 0, xh), (3, 1, zp), (4, 0, zm), (1, 1, xh)):
            xgo(i, xat(h, z, p), device, p, src(p))

    def x_forward():
        xgot(2, xat(h, zb, 0))
        xgo(6, xat(h, zb, 0), zp, 0)
        xgot(5, xat(h, zn, 1))
        xgo(7, xat(h, zn, 1), zm, 1)

    def x_pair(p):
        i, a, b = ((0, 8, 10), (1, 9, 11))[p]
        xgot(i, xat(h2, z, p))
        xgo(a, xat(h2, z, p), zp, p)
        xgo(b, xat(h2, z, p), zm, p)

    def x_forward_pair():
        xgot(8, xat(h2, zb, 0))
        xgo(12, xat(h2, zb, 0), zp, 0)
        xgot(11, xat(h2, zn, 1))
        xgo(13, xat(h2, zn, 1), zm, 1)

    slot = jnp.where(d == l, 0, 1)
    lane_row = lax.broadcasted_iota(jnp.int32, (1, 128), 1).astype(F32)

    def fill(b, carry):
        code = segb[slot, pl.ds(b, 1), :]
        other = jnp.where(lane_row == code, 0.0, 1.0).astype(BF16)
        tile = jnp.broadcast_to(other, (128, 128))
        ones = jnp.ones((128, 128), BF16)
        rows = pl.ds(pl.multiple_of((b % 4) * 128, 128), 128)
        for j in range(3):
            kvx[j, b // 4, rows, 384:512] = tile
            kvx[j, b // 4, rows, 0:128] = ones
        return carry

    def fill_q(b, carry):
        code = segb[slot, pl.ds(4 * rr + b, 1), :]
        same = jnp.where(lane_row == code, -FAR, 0.0).astype(BF16)
        tile = jnp.broadcast_to(same, (128, 128))
        rows = pl.ds(pl.multiple_of(b * 128, 128), 128)
        for j in range(3):
            qx[j, rows, 128:256] = tile
        return carry

    def start_kept():
        x_own(lambda p: mod.at[halves[p]])
        Xg[c] = mod[...]

    def start_traded():
        for p in range(2):
            net.send(swap_ids[p], mod.at[halves[p]], Xg.at[c, halves[p]], sw, lambda p=p: mod.at[halves[p]], True)
        wqkv.own_x()

    both_sides(start_kept, start_traded)
    net.recv(seg_id, segb.at[1], core)
    lax.fori_loop(0, 32, fill, 0)
    lax.fori_loop(0, 4, fill_q, 0)
    wqkv.forward()

    def kept():
        x_forward()
        wqkv.to_core()
        x_pair(0)
        wqkv.far()
        x_pair(1)
        wqkv.pair()
        x_forward_pair()
        wqkv.forward_pair()
        wqkv.pair_to_core()

    def traded():
        wqkv.pair()
        for p in range(2):
            net.recv(swap_ids[p], Xg.at[c, halves[p]], sw)
        x_own(lambda p: None)
        wqkv.to_core()
        x_forward()
        wqkv.far()
        wqkv.forward_pair()
        wqkv.pair_to_core()
        x_pair(0)
        x_pair(1)
        x_forward_pair()

    both_sides(kept, traded)
    wout.own_y()
    wout.own_x()
    wout.own_core()

    a0 = yf
    delta = (zf + 4 - yf) % 4
    third = jnp.where(delta == 0, 1, delta)
    e0 = (a0 + jnp.where(third == 1, 2, 1)) % 4
    e1 = (a0 + jnp.where(third == 3, 2, 3)) % 4
    e2 = (a0 + third) % 4

    def product(block, first, last):
        left = Xg[block]
        cols = slice(first, last)
        right = jnp.concatenate([G[2 * block, :, cols], G[2 * block + 1, :, cols]], axis=0)
        return jnp.dot(left, right, preferred_element_type=F32)

    acc[...] = jnp.zeros_like(acc)
    wqkv.near()
    for i, hh, zz, p in ((3, h, zb, 1), (4, h, zn, 0), (9, h2, zb, 1), (10, h2, zn, 0)):
        xgot(i, xat(hh, zz, p))

    def early(s, carry):
        block = 4 * (s % 2) + jnp.where(s < 2, e0, e1)
        acc[:, 0:384] += product(block, 0, 384)
        return carry

    lax.fori_loop(0, 4, early, 0)
    wqkv.far_pair()
    xgot(6, xat(h, zf, 0))
    xgot(7, xat(h, zf, 1))
    xgot(12, xat(h2, zf, 0))
    xgot(13, xat(h2, zf, 1))

    def third_blocks(s, carry):
        acc[:, 0:384] += product(4 * s + e2, 0, 384)
        return carry

    lax.fori_loop(0, 2, third_blocks, 0)
    wqkv.rest()

    power = (1.0 / HD**0.5) * math.log2(math.e)

    def rms(v):
        return v * lax.rsqrt(jnp.mean(v * v, axis=-1, keepdims=True) + EPS)

    def add_last(first, last):
        def step(s, carry):
            acc[:, first:last] += product(4 * s + a0, first, last)
            return carry

        lax.fori_loop(0, 2, step, 0)

    def add_heads(block, carry):
        acc[:, 384:1152] += product(block, 384, 1152)
        return carry

    def finish(j):
        base = 384 * j
        kvx[j, rr, :, 256:384] = rms(acc[:, base + 128 : base + 256]).astype(BF16)
        kvx[j, rr, :, 128:256] = acc[:, base + 256 : base + 384].astype(BF16)

    def finish_query(j):
        base = 384 * j
        qx[j, :, 0:128] = (rms(acc[:, base : base + 128]) * gain[j]).astype(BF16)

    ki = [net.ids(8) for _ in range(3)]

    def kat(j, yy, dd, p=None):
        rows = pl.ds(0, 512) if p is None else halves[p]
        return kvx.at[j, 2 * yy + dd, rows, pl.ds(128, 256)]

    def kgo(j, i, ref, device, p=None):
        like = lambda: kvx.at[0, 0, pl.ds(0, 512) if p is None else halves[p], pl.ds(128, 256)]
        net.send(ki[j][i], ref, ref, device, like)

    def kgot(j, i, ref):
        net.recv(ki[j][i], ref, core)

    def kv_own(j):
        me = kat(j, y, d)
        kgo(j, 0, me, yp)
        kgo(j, 1, me, ym)
        kgo(j, 2, me, core)

    def kv_forward(j):
        kgot(j, 0, kat(j, yb, d))
        kgo(j, 3, kat(j, yb, d, 0), yp, 0)
        kgo(j, 4, kat(j, yb, d), core)
        kgot(j, 1, kat(j, yn, d))
        kgo(j, 5, kat(j, yn, d, 1), ym, 1)
        kgo(j, 6, kat(j, yn, d), core)

    def attend(j, amount, row_of):
        def step(s, carry):
            key_row = row_of(s)
            rows = pl.ds(0, 512)

            @pl.when(jnp.abs(key_row - rr) <= 4)
            def _():
                scores = lax.dot_general(
                    qx[j, rows, :],
                    kvx[j, key_row, :, 256:512],
                    (((1,), (1,)), ((), ())),
                    preferred_element_type=F32,
                )
                weights = jnp.exp2(scores * power).astype(BF16)
                oacc[rows, :] += jnp.dot(
                    weights, kvx[j, key_row, :, 0:256], preferred_element_type=F32
                )

            return carry

        lax.fori_loop(0, amount, step, 0)

    def kv_far(j):
        kgot(j, 3, kat(j, yf, d, 0))
        kgot(j, 5, kat(j, yf, d, 1))
        kgo(j, 7, kat(j, yf, d), core)
        attend(j, 1, lambda k: 2 * yf + d)

    def attend_here(j):
        oacc[...] = jnp.zeros_like(oacc)
        kgot(j, 2, kat(j, y, 1 - d))
        attend(j, 2, lambda k: 2 * y + k)

    def attend_near(j):
        kgot(j, 4, kat(j, yb, 1 - d))
        kgot(j, 6, kat(j, yn, 1 - d))
        attend(j, 4, lambda k: 2 * ((y + 3 + 2 * (k // 2)) % 4) + k % 2)

    def attend_far(j):
        kgot(j, 7, kat(j, yf, 1 - d))
        attend(j, 1, lambda k: 2 * yf + 1 - d)

    ai = [net.ids(16) for _ in range(3)]

    def aat(j, hh, zz, p):
        return attg.at[j, 4 * hh + zz, halves[p]]

    def ago(j, i, hh, zz, p, device):
        net.send(ai[j][i], aat(j, hh, zz, p), aat(j, hh, zz, p), device, lambda: ast.at[0, halves[p]])

    def agot(j, i, hh, zz, p):
        net.recv(ai[j][i], aat(j, hh, zz, p), core)

    def att_send(j, p):
        for i, device in (((2, zp), (0, xh), (4, zm)), ((5, zm), (1, xh), (3, zp)))[p]:
            ago(j, i, h, z, p, device)

    def att_put(j):
        def keep(p, value):
            attg[j, c, halves[p], :] = value
            att_send(j, p)

        def swap(p, value):
            ast[j, halves[p], :] = value
            like = lambda: ast.at[0, halves[p]]
            net.send(ai[j][14 + p], ast.at[j, halves[p]], attg.at[j, c, halves[p]], sw, like, True)

        for p in range(2):
            value = (oacc[halves[p], 128:256] / oacc[halves[p], 0:128]).astype(BF16)
            pl.when(d == l)(lambda: keep(p, value))
            pl.when(d != l)(lambda: swap(p, value))

    def att_own(j):
        def traded_own():
            for p in range(2):
                agot(j, 14 + p, h, z, p)
                att_send(j, p)

        pl.when(d != l)(traded_own)

    def att_forward(j):
        agot(j, 2, h, zb, 0)
        ago(j, 6, h, zb, 0, zp)
        agot(j, 5, h, zn, 1)
        ago(j, 7, h, zn, 1, zm)
        agot(j, 0, h2, z, 0)
        ago(j, 8, h2, z, 0, zp)
        ago(j, 10, h2, z, 0, zm)
        agot(j, 1, h2, z, 1)
        ago(j, 11, h2, z, 1, zm)
        ago(j, 9, h2, z, 1, zp)

    def att_second(j):
        agot(j, 8, h2, zb, 0)
        ago(j, 12, h2, zb, 0, zp)
        agot(j, 11, h2, zn, 1)
        ago(j, 13, h2, zn, 1, zm)

    def att_rest(j):
        agot(j, 3, h, zb, 1)
        agot(j, 4, h, zn, 0)
        agot(j, 9, h2, zb, 1)
        agot(j, 10, h2, zn, 0)
        for p in range(2):
            agot(j, 6 + p, h, zf, p)
            agot(j, 12 + p, h2, zf, p)

    def wrows(block, j):
        pieces = []
        for e in range(2):
            unit = 6 * block + 2 * j + e
            pieces.append(woG[unit // 3, pl.ds(pl.multiple_of((unit % 3) * 64, 64), 64), :])
        return pieces

    def project_out(j):
        def step(p, carry):
            left = jnp.concatenate([attg[j, 2 * p], attg[j, 2 * p + 1]], axis=1)
            right = jnp.concatenate(wrows(2 * p, j) + wrows(2 * p + 1, j), axis=0)
            bacc[...] += jnp.dot(left, right, preferred_element_type=F32)
            return carry

        lax.fori_loop(0, 4, step, 0)

    add_last(128, 384)
    finish(0)
    kv_own(0)
    lax.fori_loop(0, 8, add_heads, 0)
    finish(1)
    kv_own(1)
    add_last(0, 128)
    finish(2)
    for j in range(3):
        finish_query(j)
    attend_here(0)
    kv_forward(0)
    kv_own(2)
    attend_near(0)
    kv_far(0)
    kv_forward(1)
    attend_far(0)
    att_put(0)
    attend_here(1)
    attend_near(1)
    kv_forward(2)
    att_own(0)
    wout.pair()
    wout.forward()
    kv_far(1)
    att_forward(0)
    attend_far(1)
    att_put(1)
    attend_here(2)
    attend_near(2)
    kv_far(2)
    att_own(1)
    attend_far(2)
    att_put(2)
    att_second(0)
    wout.to_core()
    att_forward(1)
    att_own(2)
    wout.far()
    wout.forward_pair()
    wout.pair_to_core()
    bacc[...] = jnp.zeros_like(bacc)
    att_second(1)
    att_rest(0)
    att_forward(2)
    wout.far_pair()
    att_second(2)
    wout.near()
    wout.rest()
    project_out(0)
    att_rest(1)
    project_out(1)
    att_rest(2)
    project_out(2)
    out[...] = (gate[...] * bacc[...]).astype(BF16)

    for i, (like, some) in net.sent.items():
        if not some:
            net.copy(i, like(), like(), core).wait_send()

    @pl.when(d != l)
    def _():
        for i, (like, some) in net.sent.items():
            if some:
                net.copy(i, like(), like(), core).wait_send()


def local(tokens, w_qkv, w_out, ada_shift, ada_scale, out_gate, head_gain, block_segment):
    vmem = pl.BlockSpec(memory_space=pltpu.VMEM)
    smem = pl.BlockSpec(memory_space=pltpu.SMEM)
    anyw = pl.BlockSpec(memory_space=pl.ANY)
    return pl.pallas_call(
        kernel,
        out_shape=jax.ShapeDtypeStruct((512, 768), BF16),
        in_specs=[anyw] * 3 + [vmem] * 3 + [smem] * 2,
        out_specs=vmem,
        scratch_shapes=[
            pltpu.VMEM((512, 768), BF16),
            pltpu.VMEM((16, 384, 1152), BF16),
            pltpu.VMEM((8, 512, 768), BF16),
            pltpu.VMEM((3, 8, 512, 512), BF16),
            pltpu.VMEM((3, 512, 256), BF16),
            pltpu.VMEM((16, 192, 768), BF16),
            pltpu.VMEM((3, 8, 512, 128), BF16),
            pltpu.VMEM((512, 1152), F32),
            pltpu.VMEM((512, 256), F32),
            pltpu.VMEM((512, 768), F32),
            pltpu.VMEM((512, 768), BF16),
            pltpu.VMEM((3, 512, 128), BF16),
            pltpu.VMEM((4, 2, 8, 512), F32),
            pltpu.VMEM((2, 32, 128), F32),
            pltpu.SemaphoreType.DMA((N_FLOWS,)),
            pltpu.SemaphoreType.DMA((N_FLOWS,)),
            pltpu.SemaphoreType.DMA((3,)),
        ],
        compiler_params=pltpu.CompilerParams(
            collective_id=0, has_side_effects=True, vmem_limit_bytes=60 * 2**20
        ),
    )(tokens, w_qkv, w_out, ada_shift, ada_scale, out_gate, head_gain, block_segment)


def solution(mesh):
    placed = (
        P(("dp", "row"), "col"),
        P(("dp", "row"), "col"),
        P(("dp", "row"), "col"),
        P("dp", None),
        P("dp", None),
        P("dp", "col"),
        P("col"),
        P("dp", None),
    )
    return jax.shard_map(
        local, mesh=mesh, in_specs=placed, out_specs=P(("dp", "row"), "col"), check_vma=False
    )
```

```python
import math

import jax
import jax.numpy as jnp
from jax import lax
from jax.experimental import pallas as pl
from jax.experimental.pallas import tpu as pltpu
from jax.sharding import PartitionSpec as P

HD = 128
BLK = 128
EPS = 1e-06
FAR = 2048.0
F32 = jnp.float32
BF16 = jnp.bfloat16
MESH = pl.DeviceIdType.MESH
N_FLOWS = 160


class Net:
    def __init__(self, ss, rs):
        self.ss, self.rs, self.count, self.sent = ss, rs, 0, {}

    def ids(self, amount):
        first = self.count
        self.count += amount
        assert self.count <= N_FLOWS
        return list(range(first, self.count))

    def copy(self, i, src, dst, device):
        return pltpu.make_async_remote_copy(
            src_ref=src,
            dst_ref=dst,
            send_sem=self.ss.at[i],
            recv_sem=self.rs.at[i],
            device_id=device,
            device_id_type=MESH,
        )

    def send(self, i, src, dst, device, like, some=False):
        self.copy(i, src, dst, device).start()
        self.sent[i] = (like, some)

    def recv(self, i, ref, device):
        self.copy(i, ref, ref, device).wait_recv()


def kernel(
    tok_hbm, wq, wo, shift, scale, gate, gain, seg, out,
    tok, G, Xg, kvx, qx, woG, attg, acc, oacc, bacc, mod, ast, st, segb, ss, rs, ls,
):
    d, row, c = lax.axis_index("dp"), lax.axis_index("row"), lax.axis_index("col")
    y, l = row // 2, row % 2
    h, z = c // 4, c % 4
    yn, yf, yb = (y + 1) % 4, (y + 2) % 4, (y + 3) % 4
    zn, zf, zb = (z + 1) % 4, (z + 2) % 4, (z + 3) % 4
    h2 = 1 - h
    core = (1 - d, row, c)
    xl = (d, 2 * y + 1 - l, c)
    yp, ym = (d, 2 * yn + l, c), (d, 2 * yb + l, c)
    zp, zm = (d, row, 4 * h + zn), (d, row, 4 * h + zb)
    xh = (d, row, 4 * h2 + z)
    sw = (l, 2 * y + d, c)
    rr = 2 * y + d
    net = Net(ss, rs)

    def both_sides(first, second):
        pl.when(d == l)(first)
        pl.when(d != l)(second)

    tok_copy = pltpu.make_async_copy(tok_hbm, tok, ls.at[2])
    tok_copy.start()

    barrier = pltpu.get_barrier_semaphore()
    z_peers = [(d, row, 4 * h + (z + k) % 4) for k in range(1, 4)]
    for peer in z_peers + [xh, core, xl, yp, ym]:
        pl.semaphore_signal(barrier, inc=1, device_id=peer, device_id_type=MESH)

    @pl.when(d != l)
    def _():
        pl.semaphore_signal(barrier, inc=1, device_id=sw, device_id_type=MESH)

    for b in range(32):
        segb[0, b : b + 1, :] = jnp.full((1, 128), seg[0, b], jnp.int32).astype(F32)

    tok_copy.wait()
    x = tok[...].astype(F32)
    part_mean = jnp.sum(x, axis=-1, keepdims=True) * (1.0 / 768.0)
    off = x - part_mean
    part_sq = jnp.sum(off * off, axis=-1, keepdims=True)
    lane = lax.broadcasted_iota(jnp.int32, (512, 128), 1)
    columns = jnp.where(lane == 0, part_mean, jnp.where(lane == 1, part_sq, 0.0))
    st[z, h] = columns.T[:8]
    pl.semaphore_wait(barrier, 8 + (d + l) % 2)

    def wid(dd, yy, ll):
        return 8 * dd + 2 * yy + ll

    class Weight:
        def __init__(self, src, dst, rows, local_sem):
            self.src, self.dst, self.half = src, dst, rows // 2
            self.parts = {None: pl.ds(0, rows), 0: pl.ds(0, rows // 2), 1: pl.ds(rows // 2, rows // 2)}
            self.f = dict(zip(self.names, net.ids(len(self.names))))
            self.local = pltpu.make_async_copy(src, dst.at[wid(d, y, l)], local_sem)

        names = (
            "own_yp0", "own_yp1", "own_ym0", "own_ym1", "own_xl0", "own_xl1",
            "own_core", "fwd_yp", "fwd_ym", "core_yb", "core_yn", "pair_yp0",
            "pair_yp1", "pair_ym0", "pair_ym1", "core_pair", "last_yp", "last_ym",
            "core_yb2", "core_yn2", "far0", "far1", "far2", "far3",
        )

        def at(self, dd, yy, ll, part=None):
            return self.dst.at[wid(dd, yy, ll), self.parts[part]]

        def go(self, name, device, dd, yy, ll, part=None, src=None):
            ref = self.at(dd, yy, ll, part)
            like = lambda: self.dst.at[0, self.parts[part]]
            net.send(self.f[name], ref if src is None else src, ref, device, like)

        def got(self, name, dd, yy, ll, part=None):
            net.recv(self.f[name], self.at(dd, yy, ll, part), core)

        def own(self, name, device, part=None):
            self.go(name, device, d, y, l, part, self.src.at[self.parts[part]])

        def own_y(self):
            self.own("own_yp0", yp, 0)
            self.own("own_ym1", ym, 1)
            self.own("own_yp1", yp, 1)
            self.own("own_ym0", ym, 0)

        def own_core(self):
            self.own("own_core", core)
            self.local.start()

        def own_x(self):
            self.own("own_xl0", xl, 0)
            self.own("own_xl1", xl, 1)

        def forward(self):
            self.got("own_yp0", d, yb, l, 0)
            self.go("fwd_yp", yp, d, yb, l, 0)
            self.got("own_ym1", d, yn, l, 1)
            self.go("fwd_ym", ym, d, yn, l, 1)

        def to_core(self):
            self.got("own_yp1", d, yb, l, 1)
            self.go("core_yb", core, d, yb, l)
            self.got("own_ym0", d, yn, l, 0)
            self.go("core_yn", core, d, yn, l)

        def pair(self):
            for p in range(2):
                self.got(f"own_xl{p}", d, y, 1 - l, p)
                self.go(f"pair_yp{p}", yp, d, y, 1 - l, p)
                self.go(f"pair_ym{p}", ym, d, y, 1 - l, p)
            self.go("core_pair", core, d, y, 1 - l)

        def forward_pair(self):
            self.got("pair_yp0", d, yb, 1 - l, 0)
            self.go("last_yp", yp, d, yb, 1 - l, 0)
            self.got("pair_ym1", d, yn, 1 - l, 1)
            self.go("last_ym", ym, d, yn, 1 - l, 1)

        def pair_to_core(self):
            self.got("pair_yp1", d, yb, 1 - l, 1)
            self.go("core_yb2", core, d, yb, 1 - l)
            self.got("pair_ym0", d, yn, 1 - l, 0)
            self.go("core_yn2", core, d, yn, 1 - l)

        def far(self):
            self.got("fwd_yp", d, yf, l, 0)
            self.go("far0", core, d, yf, l, 0)
            self.got("fwd_ym", d, yf, l, 1)
            self.go("far1", core, d, yf, l, 1)

        def far_pair(self):
            self.got("last_yp", d, yf, 1 - l, 0)
            self.go("far2", core, d, yf, 1 - l, 0)
            self.got("last_ym", d, yf, 1 - l, 1)
            self.go("far3", core, d, yf, 1 - l, 1)

        def near(self):
            self.local.wait()
            self.got("own_core", 1 - d, y, l)
            self.got("core_yb", 1 - d, yb, l)
            self.got("core_yn", 1 - d, yn, l)
            self.got("core_pair", 1 - d, y, 1 - l)
            self.got("core_yb2", 1 - d, yb, 1 - l)
            self.got("core_yn2", 1 - d, yn, 1 - l)

        def rest(self):
            for p in range(2):
                self.got(f"far{p}", 1 - d, yf, l, p)
                self.got(f"far{2 + p}", 1 - d, yf, 1 - l, p)

    wqkv = Weight(wq, G, 384, ls.at[0])
    wout = Weight(wo, woG, 192, ls.at[1])

    st_ids = net.ids(4)
    net.send(st_ids[0], st.at[z, h], st.at[z, h], xh, lambda: st.at[0, 0])
    seg_id = net.ids(1)[0]
    net.send(seg_id, segb.at[0], segb.at[1], core, lambda: segb.at[0])
    wqkv.own_y()
    pl.when(d == l)(wqkv.own_x)
    wqkv.own_core()
    net.recv(st_ids[0], st.at[z, h2], xh)
    for k in range(1, 4):
        net.send(st_ids[k], st.at[z], st.at[z], z_peers[k - 1], lambda: st.at[0])
    for k in range(1, 4):
        net.recv(st_ids[k], st.at[(z + 4 - k) % 4], core)
    means = [st[k // 2, k % 2, 0:1, :] for k in range(8)]
    mean = sum(means) * 0.125
    total_sq = sum(st[k // 2, k % 2, 1:2, :] for k in range(8))
    total_sq = total_sq + 768.0 * sum((m - mean) * (m - mean) for m in means)
    inv = lax.rsqrt(total_sq * (1.0 / 6144.0) + EPS)
    sub = lax.broadcasted_iota(jnp.int32, (128, 512), 0)
    columns = jnp.where(sub == 0, mean, jnp.where(sub == 1, inv, 0.0)).T
    lanes = pl.ds(pl.multiple_of(c * 768, 768), 768)
    normed = (tok[...].astype(F32) - columns[:, 0:1]) * columns[:, 1:2]
    modulated = (normed * (1.0 + scale[0:1, lanes]) + shift[0:1, lanes]).astype(BF16)
    mod[...] = modulated
    swap_ids = net.ids(2)
    halves = (pl.ds(0, 256), pl.ds(256, 256))

    xi = net.ids(14)

    def xat(hh, zz, p):
        return Xg.at[4 * hh + zz, halves[p]]

    def xgo(i, ref, device, p, src=None):
        net.send(xi[i], ref if src is None else src, ref, device, lambda: mod.at[halves[p]])

    def xgot(i, ref):
        net.recv(xi[i], ref, core)

    def x_own(src):
        for i, p, device in ((2, 0, zp), (5, 1, zm), (0, 0, xh), (3, 1, zp), (4, 0, zm), (1, 1, xh)):
            xgo(i, xat(h, z, p), device, p, src(p))

    def x_forward():
        xgot(2, xat(h, zb, 0))
        xgo(6, xat(h, zb, 0), zp, 0)
        xgot(5, xat(h, zn, 1))
        xgo(7, xat(h, zn, 1), zm, 1)

    def x_pair(p):
        i, a, b = ((0, 8, 10), (1, 9, 11))[p]
        xgot(i, xat(h2, z, p))
        xgo(a, xat(h2, z, p), zp, p)
        xgo(b, xat(h2, z, p), zm, p)

    def x_forward_pair():
        xgot(8, xat(h2, zb, 0))
        xgo(12, xat(h2, zb, 0), zp, 0)
        xgot(11, xat(h2, zn, 1))
        xgo(13, xat(h2, zn, 1), zm, 1)

    slot = jnp.where(d == l, 0, 1)
    lane_row = lax.broadcasted_iota(jnp.int32, (1, 128), 1).astype(F32)

    def fill(b, carry):
        code = segb[slot, pl.ds(b, 1), :]
        other = jnp.where(lane_row == code, 0.0, 1.0).astype(BF16)
        tile = jnp.broadcast_to(other, (128, 128))
        ones = jnp.ones((128, 128), BF16)
        rows = pl.ds(pl.multiple_of((b % 4) * 128, 128), 128)
        for j in range(3):
            kvx[j, b // 4, rows, 384:512] = tile
            kvx[j, b // 4, rows, 0:128] = ones
        return carry

    def fill_q(b, carry):
        code = segb[slot, pl.ds(4 * rr + b, 1), :]
        same = jnp.where(lane_row == code, -FAR, 0.0).astype(BF16)
        tile = jnp.broadcast_to(same, (128, 128))
        rows = pl.ds(pl.multiple_of(b * 128, 128), 128)
        for j in range(3):
            qx[j, rows, 128:256] = tile
        return carry

    def start_kept():
        x_own(lambda p: mod.at[halves[p]])
        Xg[c] = mod[...]

    def start_traded():
        for p in range(2):
            net.send(swap_ids[p], mod.at[halves[p]], Xg.at[c, halves[p]], sw, lambda p=p: mod.at[halves[p]], True)
        wqkv.own_x()

    both_sides(start_kept, start_traded)
    net.recv(seg_id, segb.at[1], core)
    lax.fori_loop(0, 32, fill, 0)
    lax.fori_loop(0, 4, fill_q, 0)
    wqkv.forward()

    def kept():
        x_forward()
        wqkv.to_core()
        x_pair(0)
        wqkv.far()
        x_pair(1)
        wqkv.pair()
        x_forward_pair()
        wqkv.forward_pair()
        wqkv.pair_to_core()

    def traded():
        wqkv.pair()
        for p in range(2):
            net.recv(swap_ids[p], Xg.at[c, halves[p]], sw)
        x_own(lambda p: None)
        wqkv.to_core()
        x_forward()
        wqkv.far()
        wqkv.forward_pair()
        wqkv.pair_to_core()
        x_pair(0)
        x_pair(1)
        x_forward_pair()

    both_sides(kept, traded)
    wout.own_y()
    wout.own_x()
    wout.own_core()

    a0 = yf
    delta = (zf + 4 - yf) % 4
    third = jnp.where(delta == 0, 1, delta)
    e0 = (a0 + jnp.where(third == 1, 2, 1)) % 4
    e1 = (a0 + jnp.where(third == 3, 2, 3)) % 4
    e2 = (a0 + third) % 4

    def product(block, first, last):
        left = Xg[block]
        cols = slice(first, last)
        right = jnp.concatenate([G[2 * block, :, cols], G[2 * block + 1, :, cols]], axis=0)
        return jnp.dot(left, right, preferred_element_type=F32)

    acc[...] = jnp.zeros_like(acc)
    wqkv.near()
    for i, hh, zz, p in ((3, h, zb, 1), (4, h, zn, 0), (9, h2, zb, 1), (10, h2, zn, 0)):
        xgot(i, xat(hh, zz, p))

    def early(s, carry):
        block = 4 * (s % 2) + jnp.where(s < 2, e0, e1)
        acc[:, 0:384] += product(block, 0, 384)
        return carry

    lax.fori_loop(0, 4, early, 0)
    wqkv.far_pair()
    xgot(6, xat(h, zf, 0))
    xgot(7, xat(h, zf, 1))
    xgot(12, xat(h2, zf, 0))
    xgot(13, xat(h2, zf, 1))

    def third_blocks(s, carry):
        acc[:, 0:384] += product(4 * s + e2, 0, 384)
        return carry

    lax.fori_loop(0, 2, third_blocks, 0)
    wqkv.rest()

    power = (1.0 / HD**0.5) * math.log2(math.e)

    def rms(v):
        return v * lax.rsqrt(jnp.mean(v * v, axis=-1, keepdims=True) + EPS)

    def add_last(first, last):
        def step(s, carry):
            acc[:, first:last] += product(4 * s + a0, first, last)
            return carry

        lax.fori_loop(0, 2, step, 0)

    def add_heads(block, carry):
        acc[:, 384:1152] += product(block, 384, 1152)
        return carry

    def finish(j):
        base = 384 * j
        kvx[j, rr, :, 256:384] = rms(acc[:, base + 128 : base + 256]).astype(BF16)
        kvx[j, rr, :, 128:256] = acc[:, base + 256 : base + 384].astype(BF16)

    def finish_query(j):
        base = 384 * j
        qx[j, :, 0:128] = (rms(acc[:, base : base + 128]) * gain[j]).astype(BF16)

    ki = [net.ids(8) for _ in range(3)]

    def kat(j, yy, dd, p=None):
        rows = pl.ds(0, 512) if p is None else halves[p]
        return kvx.at[j, 2 * yy + dd, rows, pl.ds(128, 256)]

    def kgo(j, i, ref, device, p=None):
        like = lambda: kvx.at[0, 0, pl.ds(0, 512) if p is None else halves[p], pl.ds(128, 256)]
        net.send(ki[j][i], ref, ref, device, like)

    def kgot(j, i, ref):
        net.recv(ki[j][i], ref, core)

    def kv_own(j):
        me = kat(j, y, d)
        kgo(j, 0, me, yp)
        kgo(j, 1, me, ym)
        kgo(j, 2, me, core)

    def kv_forward(j):
        kgot(j, 0, kat(j, yb, d))
        kgo(j, 3, kat(j, yb, d, 0), yp, 0)
        kgo(j, 4, kat(j, yb, d), core)
        kgot(j, 1, kat(j, yn, d))
        kgo(j, 5, kat(j, yn, d, 1), ym, 1)
        kgo(j, 6, kat(j, yn, d), core)

    def attend(j, amount, row_of):
        def step(s, carry):
            key_row = row_of(s)
            rows = pl.ds(0, 512)

            @pl.when(jnp.abs(key_row - rr) <= 4)
            def _():
                scores = lax.dot_general(
                    qx[j, rows, :],
                    kvx[j, key_row, :, 256:512],
                    (((1,), (1,)), ((), ())),
                    preferred_element_type=F32,
                )
                weights = jnp.exp2(scores * power).astype(BF16)
                oacc[rows, :] += jnp.dot(
                    weights, kvx[j, key_row, :, 0:256], preferred_element_type=F32
                )

            return carry

        lax.fori_loop(0, amount, step, 0)

    def kv_far(j):
        kgot(j, 3, kat(j, yf, d, 0))
        kgot(j, 5, kat(j, yf, d, 1))
        kgo(j, 7, kat(j, yf, d), core)
        attend(j, 1, lambda k: 2 * yf + d)

    def attend_here(j):
        oacc[...] = jnp.zeros_like(oacc)
        kgot(j, 2, kat(j, y, 1 - d))
        attend(j, 2, lambda k: 2 * y + k)

    def attend_near(j):
        attend(j, 2, lambda k: 2 * ((y + 3 + 2 * k) % 4) + d)
        kgot(j, 4, kat(j, yb, 1 - d))
        kgot(j, 6, kat(j, yn, 1 - d))
        attend(j, 2, lambda k: 2 * ((y + 3 + 2 * k) % 4) + 1 - d)

    def attend_far(j):
        kgot(j, 7, kat(j, yf, 1 - d))
        attend(j, 1, lambda k: 2 * yf + 1 - d)

    ai = [net.ids(16) for _ in range(3)]

    def aat(j, hh, zz, p):
        return attg.at[j, 4 * hh + zz, halves[p]]

    def ago(j, i, hh, zz, p, device):
        net.send(ai[j][i], aat(j, hh, zz, p), aat(j, hh, zz, p), device, lambda: ast.at[0, halves[p]])

    def agot(j, i, hh, zz, p):
        net.recv(ai[j][i], aat(j, hh, zz, p), core)

    def att_send(j, p):
        for i, device in (((2, zp), (0, xh), (4, zm)), ((5, zm), (1, xh), (3, zp)))[p]:
            ago(j, i, h, z, p, device)

    def att_put(j):
        def keep(p, value):
            attg[j, c, halves[p], :] = value
            att_send(j, p)

        def swap(p, value):
            ast[j, halves[p], :] = value
            like = lambda: ast.at[0, halves[p]]
            net.send(ai[j][14 + p], ast.at[j, halves[p]], attg.at[j, c, halves[p]], sw, like, True)

        for p in range(2):
            value = (oacc[halves[p], 128:256] / oacc[halves[p], 0:128]).astype(BF16)
            pl.when(d == l)(lambda: keep(p, value))
            pl.when(d != l)(lambda: swap(p, value))

    def att_own(j):
        def traded_own():
            for p in range(2):
                agot(j, 14 + p, h, z, p)
                att_send(j, p)

        pl.when(d != l)(traded_own)

    def att_forward(j):
        agot(j, 2, h, zb, 0)
        ago(j, 6, h, zb, 0, zp)
        agot(j, 5, h, zn, 1)
        ago(j, 7, h, zn, 1, zm)
        agot(j, 0, h2, z, 0)
        ago(j, 8, h2, z, 0, zp)
        ago(j, 10, h2, z, 0, zm)
        agot(j, 1, h2, z, 1)
        ago(j, 11, h2, z, 1, zm)
        ago(j, 9, h2, z, 1, zp)

    def att_second(j):
        agot(j, 8, h2, zb, 0)
        ago(j, 12, h2, zb, 0, zp)
        agot(j, 11, h2, zn, 1)
        ago(j, 13, h2, zn, 1, zm)

    def att_rest(j):
        agot(j, 3, h, zb, 1)
        agot(j, 4, h, zn, 0)
        agot(j, 9, h2, zb, 1)
        agot(j, 10, h2, zn, 0)
        for p in range(2):
            agot(j, 6 + p, h, zf, p)
            agot(j, 12 + p, h2, zf, p)

    def wrows(block, j):
        pieces = []
        for e in range(2):
            unit = 6 * block + 2 * j + e
            pieces.append(woG[unit // 3, pl.ds(pl.multiple_of((unit % 3) * 64, 64), 64), :])
        return pieces

    def project_out(j):
        def step(p, carry):
            left = jnp.concatenate([attg[j, 2 * p], attg[j, 2 * p + 1]], axis=1)
            right = jnp.concatenate(wrows(2 * p, j) + wrows(2 * p + 1, j), axis=0)
            bacc[...] += jnp.dot(left, right, preferred_element_type=F32)
            return carry

        lax.fori_loop(0, 4, step, 0)

    add_last(128, 384)
    finish(0)
    kv_own(0)
    lax.fori_loop(0, 8, add_heads, 0)
    finish(1)
    kv_own(1)
    add_last(0, 128)
    finish(2)
    for j in range(3):
        finish_query(j)
    attend_here(0)
    kv_forward(0)
    kv_own(2)
    attend_near(0)
    kv_far(0)
    kv_forward(1)
    attend_far(0)
    att_put(0)
    attend_here(1)
    attend_near(1)
    kv_forward(2)
    att_own(0)
    wout.pair()
    wout.forward()
    kv_far(1)
    att_forward(0)
    attend_far(1)
    att_put(1)
    attend_here(2)
    attend_near(2)
    kv_far(2)
    att_own(1)
    attend_far(2)
    att_put(2)
    att_second(0)
    wout.to_core()
    att_forward(1)
    att_own(2)
    wout.far()
    wout.forward_pair()
    wout.pair_to_core()
    bacc[...] = jnp.zeros_like(bacc)
    att_second(1)
    att_rest(0)
    att_forward(2)
    wout.far_pair()
    att_second(2)
    wout.near()
    wout.rest()
    project_out(0)
    att_rest(1)
    project_out(1)
    att_rest(2)
    project_out(2)
    out[...] = (gate[...] * bacc[...]).astype(BF16)

    for i, (like, some) in net.sent.items():
        if not some:
            net.copy(i, like(), like(), core).wait_send()

    @pl.when(d != l)
    def _():
        for i, (like, some) in net.sent.items():
            if some:
                net.copy(i, like(), like(), core).wait_send()


def local(tokens, w_qkv, w_out, ada_shift, ada_scale, out_gate, head_gain, block_segment):
    vmem = pl.BlockSpec(memory_space=pltpu.VMEM)
    smem = pl.BlockSpec(memory_space=pltpu.SMEM)
    anyw = pl.BlockSpec(memory_space=pl.ANY)
    return pl.pallas_call(
        kernel,
        out_shape=jax.ShapeDtypeStruct((512, 768), BF16),
        in_specs=[anyw] * 3 + [vmem] * 3 + [smem] * 2,
        out_specs=vmem,
        scratch_shapes=[
            pltpu.VMEM((512, 768), BF16),
            pltpu.VMEM((16, 384, 1152), BF16),
            pltpu.VMEM((8, 512, 768), BF16),
            pltpu.VMEM((3, 8, 512, 512), BF16),
            pltpu.VMEM((3, 512, 256), BF16),
            pltpu.VMEM((16, 192, 768), BF16),
            pltpu.VMEM((3, 8, 512, 128), BF16),
            pltpu.VMEM((512, 1152), F32),
            pltpu.VMEM((512, 256), F32),
            pltpu.VMEM((512, 768), F32),
            pltpu.VMEM((512, 768), BF16),
            pltpu.VMEM((3, 512, 128), BF16),
            pltpu.VMEM((4, 2, 8, 512), F32),
            pltpu.VMEM((2, 32, 128), F32),
            pltpu.SemaphoreType.DMA((N_FLOWS,)),
            pltpu.SemaphoreType.DMA((N_FLOWS,)),
            pltpu.SemaphoreType.DMA((3,)),
        ],
        compiler_params=pltpu.CompilerParams(
            collective_id=0, has_side_effects=True, vmem_limit_bytes=60 * 2**20
        ),
    )(tokens, w_qkv, w_out, ada_shift, ada_scale, out_gate, head_gain, block_segment)


def solution(mesh):
    placed = (
        P(("dp", "row"), "col"),
        P(("dp", "row"), "col"),
        P(("dp", "row"), "col"),
        P("dp", None),
        P("dp", None),
        P("dp", "col"),
        P("col"),
        P("dp", None),
    )
    return jax.shard_map(
        local, mesh=mesh, in_specs=placed, out_specs=P(("dp", "row"), "col"), check_vma=False
    )
```
